256 devices in a mesh: seq: 64 (over y, z, core), head: 4 (over x).
Axes of the slice: x: 4, y: 4, z: 8, core: 2. Of those that a mesh axis runs over, the one named last changes fastest.
Arguments:
- x_in: bfloat16 [32768, 4096], P('seq', 'head'), may hold values from -160 to 160
- gate_in: bfloat16 [32768, 4096], P('seq', 'head'), may hold values from -6 to 6
- bc_in: bfloat16 [32768, 256], P('seq'), may hold values from -2.390625 to 2.390625
- step_in: float32 [32768, 64], P('seq', 'head'), may hold values from 0.005 to 0.05
- decay_code: int32 [2, 32768, 64], P(None, 'seq', 'head'), may hold values from 1 to 131072
- decay_rate: float32 [2, 64], P(None, 'head'), may hold values from 1.8310547e-06 to 0.012
- skip_gain: float32 [2, 64], P(None, 'head'), may hold values from 0.25 to 1.5
- norm_gain: float32 [4096], P('head'), may hold values from 0.1 to 1.9
- w_out: bfloat16 [4096, 4096], P('head', 'seq'), may hold values from -0.09375 to 0.09375
- resid_in: bfloat16 [32768, 4096], P('seq', 'head'), may hold values from -25 to 25
- resid_gain: float32 [4096], replicated, may hold values from 0.1 to 1.9
- w_in_x: bfloat16 [4096, 4096], P('seq', 'head'), may hold values from -1 to 1
- w_in_bc: bfloat16 [4096, 256], P('seq'), may hold values from -0.09375 to 0.09375
- w_in_dt: bfloat16 [4096, 64], P('seq', 'head'), may hold values from -0.09375 to 0.09375
- step_time_bias: float32 [64], P('head'), may hold values from -3 to -1
- conv_x: bfloat16 [4, 4096], P(None, 'head'), may hold values from -3 to 3
- conv_bc: bfloat16 [4, 256], replicated, may hold values from -3 to 3
Outputs:
- resid_out: bfloat16 [32768, 4096], P('seq', 'head')
- mixer_out: bfloat16 [32768, 4096], P('seq', 'head')
The draws below stay inside these ranges and needn't reach their ends.
All inputs are finite; a program needn't handle non-finite values.
Results may differ from the reference program's by a relative error of at most 0.007.
Values may be sent and summed in bfloat16 or wider, within the bound.
A program may use at most 128 MiB of HBM per device.

```python
import math
import jax
import jax.numpy as jnp
from jax import lax

D = 4096
HEADS = 64
HEAD_CHANNELS = 64
STATE = 128
GROUP = 256
CONV = 4
INNER = 4096
SEQUENCE_TOKENS = 32768


def rough_scale(key, count, spread):
    return 10.0 ** jax.random.uniform(key, (count,), jnp.float32, -spread, spread)


def base_values(key, shape):
    return jax.random.truncated_normal(key, -4.0, 4.0, shape, jnp.float32)


def draw_x_in(key, part):
    keys = jax.random.split(key, 3)
    values = base_values(keys[0], (SEQUENCE_TOKENS, INNER))
    row_scale = rough_scale(keys[1], SEQUENCE_TOKENS, 0.5)
    rising = 3.0 ** (jnp.arange(INNER, dtype=jnp.float32) / (INNER - 1))
    column_factor = rough_scale(keys[2], INNER, 0.5) * rising
    values = values * row_scale[:, None] * column_factor[None, :]
    return jnp.clip(values, -160.0, 160.0).astype(jnp.bfloat16)


def draw_resid_in(key, part):
    keys = jax.random.split(key, 3)
    values = base_values(keys[0], (SEQUENCE_TOKENS, D))
    row_scale = rough_scale(keys[1], SEQUENCE_TOKENS, 0.5)
    rising = 3.0 ** (jnp.arange(D, dtype=jnp.float32) / (D - 1)) / 1.7
    column_factor = rough_scale(keys[2], D, 0.5) * rising
    values = values * row_scale[:, None] * column_factor[None, :]
    return jnp.clip(values, -25.0, 25.0).astype(jnp.bfloat16)


def draw_w_in_x(key, part):
    keys = jax.random.split(key, 2)
    values = base_values(keys[0], (D, INNER)) * D ** (-0.5)
    rising = 3.0 ** (jnp.arange(INNER, dtype=jnp.float32) / (INNER - 1))
    column_factor = rough_scale(keys[1], INNER, 0.5) * rising
    values = values * column_factor[None, :]
    return jnp.clip(values, -1.0, 1.0).astype(jnp.bfloat16)


def draw_decay_code(key, part):
    keys = jax.random.split(key, 3)
    block_count = SEQUENCE_TOKENS // GROUP
    level = jax.random.randint(keys[0], (2, block_count, 1), 1, 3) * 2
    level = jnp.repeat(level, GROUP, axis=1)
    decay_labels = jax.random.randint(keys[1], (2, SEQUENCE_TOKENS, HEADS), 1, 2 * level)
    device_spots = jax.random.randint(keys[2], (2, 2), 0, SEQUENCE_TOKENS)
    transfer_group = jnp.any(jnp.arange(SEQUENCE_TOKENS, dtype=jnp.int32)[None, None, :] == device_spots[:, :, None], axis=1)
    return jnp.where(transfer_group[:, :, None], 4 * SEQUENCE_TOKENS, decay_labels).astype(jnp.int32)


def draw_decay_rate(key, part):
    keys = jax.random.split(key, 3)
    share = 0.5
    slow_pick = jax.random.uniform(keys[0], (2, HEADS), jnp.float32) < share
    slow_rate = jnp.exp(jax.random.uniform(keys[1], (2, HEADS), jnp.float32, math.log(0.25), math.log(0.6))) / (4.0 * SEQUENCE_TOKENS)
    fast_rate = jnp.exp(jax.random.uniform(keys[2], (2, HEADS), jnp.float32, math.log(0.006), math.log(0.012)))
    return jnp.where(slow_pick, slow_rate, fast_rate).astype(jnp.float32)


def steps_of(rng, extent, cuts, smallest, largest):
    def one(position, blocks):
        draws = jax.random.uniform(jax.random.fold_in(jax.random.fold_in(rng, 6), position), (blocks,), jnp.float32, smallest / len(cuts), largest / len(cuts))
        return jnp.repeat(jnp.exp(draws), extent[position] // blocks).reshape((-1,) + (1,) * (len(extent) - position - 1))

    factor_of = one(*cuts[0])
    for cut in cuts[1:]:
        factor_of = factor_of * one(*cut)
    return factor_of


def bell_draw(rng, shape, scale, bound, pieces=(), held_as=jnp.bfloat16):
    drawn = scale * jax.random.normal(rng, shape, jnp.float32)
    if pieces:
        drawn = drawn * steps_of(rng, shape, pieces, -0.22, 0.18)
    return jnp.clip(drawn, -bound, bound).astype(held_as)


def setup_inputs(seed: int = 0) -> dict:
    arg_keys = jax.random.split(jax.random.key(seed), 18)
    return {
        "x_in": draw_x_in(jax.random.fold_in(arg_keys[17], 71), 0),
        "gate_in": bell_draw(arg_keys[1], (SEQUENCE_TOKENS, INNER), 1.0, 6.0, ((0, 64), (1, 4))),
        "bc_in": bell_draw(arg_keys[2], (SEQUENCE_TOKENS, 2 * STATE), 0.3, 2.390625, ((0, 64),)),
        "step_in": jnp.clip(jnp.exp(math.log(0.05) - 2.3025851 * jax.random.uniform(arg_keys[3], (SEQUENCE_TOKENS, HEADS), jnp.float32) ** steps_of(arg_keys[3], (SEQUENCE_TOKENS, HEADS), ((0, 64), (1, 4)), -0.2, 0.2)), 0.005, 0.05),
        "decay_code": draw_decay_code(jax.random.fold_in(arg_keys[17], 71), 0),
        "decay_rate": draw_decay_rate(jax.random.fold_in(arg_keys[17], 71), 0),
        "skip_gain": jnp.clip(0.25 + 1.25 * jax.random.uniform(arg_keys[6], (2, HEADS), jnp.float32) ** steps_of(arg_keys[6], (2, HEADS), ((1, 4),), -0.2, 0.2), 0.25, 1.5),
        "norm_gain": jnp.clip(1.0 + 0.18 * jax.random.normal(arg_keys[7], (INNER,), jnp.float32), 0.1, 1.9),
        "w_out": bell_draw(arg_keys[8], (INNER, D), INNER ** -0.5, 0.09375, ((0, 4), (1, 64))),
        "resid_in": draw_resid_in(jax.random.fold_in(arg_keys[17], 71), 0),
        "resid_gain": jnp.clip(1.0 + 0.18 * jax.random.normal(arg_keys[10], (D,), jnp.float32), 0.1, 1.9),
        "w_in_x": draw_w_in_x(jax.random.fold_in(arg_keys[17], 71), 0),
        "w_in_bc": bell_draw(arg_keys[12], (D, 2 * STATE), D ** -0.5, 0.09375, ((0, 64),)),
        "w_in_dt": bell_draw(arg_keys[13], (D, HEADS), D ** -0.5, 0.09375, ((0, 64), (1, 4))),
        "step_time_bias": jnp.clip(-3.0 + 2.0 * jax.random.uniform(arg_keys[14], (HEADS,), jnp.float32) ** steps_of(arg_keys[14], (HEADS,), ((0, 4),), -0.2, 0.2), -3.0, -1.0),
        "conv_x": bell_draw(arg_keys[15], (CONV, INNER), CONV ** -0.5, 3.0, ((1, 4),)),
        "conv_bc": bell_draw(arg_keys[16], (CONV, 2 * STATE), CONV ** -0.5, 3.0),
    }


def log_decay(decay_labels, rates):
    return -jnp.minimum(decay_labels.astype(jnp.float32) * rates[None, :], 20.0)

def group_terms(input_block, b_block, c_block, step_block, decay_block):
    length = input_block.shape[0]
    head_count = step_block.shape[1]
    input_heads = input_block.reshape(length, head_count, HEAD_CHANNELS)
    cumulative = jnp.cumsum(decay_block, axis=0)
    across = cumulative.T
    segment = across[:, :, None] - across[:, None, :]
    lower_mask = (lax.broadcasted_iota(jnp.int32, (length, length), 0) >= lax.broadcasted_iota(jnp.int32, (length, length), 1))[None, :, :]
    scores = jnp.dot(c_block, b_block.T, preferred_element_type=jnp.float32)
    weights_mix = (jnp.where(lower_mask, jnp.exp(jnp.minimum(segment, 0.0)), 0.0) * scores[None, :, :] * step_block.T[:, None, :]).astype(jnp.bfloat16)
    diag_part = jnp.einsum('hij,jhp->ihp', weights_mix.astype(jnp.float32), input_heads.astype(jnp.float32))
    end_weight = jnp.exp(cumulative[-1][None, :] - cumulative) * step_block
    scaled_input = (input_heads.astype(jnp.float32) * end_weight[:, :, None]).astype(jnp.bfloat16)
    local_state = jnp.einsum('jhp,jn->hpn', scaled_input.astype(jnp.float32), b_block.astype(jnp.float32))
    return (diag_part, cumulative, local_state, cumulative[-1])

def ssd_layer(inputs, bc_values, step_values, decay_values, skip_values):
    state_width = bc_values.shape[1] // 2
    head_count = step_values.shape[1]
    token_count = inputs.shape[0]
    block_count = token_count // GROUP

    def advance(carry_state, block_data):
        input_block, bc_block, step_block, decay_block = block_data
        c_block = bc_block[:, state_width:]
        diag_part, cumulative, local_state, total_decay = group_terms(input_block, bc_block[:, :state_width], c_block, step_block, decay_block)
        carried_part = jnp.einsum('in,hpn->ihp', c_block.astype(jnp.float32), carry_state, precision=lax.Precision.HIGH) * jnp.exp(cumulative)[:, :, None]
        next_state = jnp.exp(total_decay)[:, None, None] * carry_state + local_state
        return (next_state, diag_part + carried_part)
    blocks = (inputs.reshape(block_count, GROUP, inputs.shape[1]), bc_values.reshape(block_count, GROUP, bc_values.shape[1]), step_values.reshape(block_count, GROUP, head_count), decay_values.reshape(block_count, GROUP, head_count))
    initial = jnp.zeros((head_count, HEAD_CHANNELS, state_width), jnp.float32)
    final_state, outputs = lax.scan(advance, initial, blocks)
    mixed = outputs.reshape(token_count, head_count, HEAD_CHANNELS)
    mixed = mixed + skip_values[None, :, None] * inputs.reshape(token_count, head_count, HEAD_CHANNELS).astype(jnp.float32)
    return mixed.reshape(token_count, head_count * HEAD_CHANNELS)

def rms_scale(values):
    return lax.rsqrt(lax.optimization_barrier(jnp.mean(values * values, axis=1, keepdims=True)) + 1e-05)

def causal_conv(padded, kernel, length):
    total = padded[0:length].astype(jnp.float32) * kernel[0].astype(jnp.float32)[None, :]
    for tap_index in range(1, kernel.shape[0]):
        total = total + padded[tap_index:tap_index + length].astype(jnp.float32) * kernel[tap_index].astype(jnp.float32)[None, :]
    return total

def reference(x_in, gate_in, bc_in, step_in, decay_code, decay_rate, skip_gain, norm_gain, w_out, resid_in, resid_gain, w_in_x, w_in_bc, w_in_dt, step_time_bias, conv_x, conv_bc):
    token_count = x_in.shape[0]
    decay_one = log_decay(decay_code[0], decay_rate[0])
    mixed_one = ssd_layer(x_in, bc_in, step_in, decay_one, skip_gain[0])
    gated = mixed_one * jax.nn.silu(gate_in.astype(jnp.float32))
    normed = (gated * rms_scale(gated) * norm_gain[None, :]).astype(jnp.bfloat16)
    resid_out = (resid_in.astype(jnp.float32) + jnp.dot(normed, w_out, preferred_element_type=jnp.float32)).astype(jnp.bfloat16)
    hidden = resid_out.astype(jnp.float32)
    hidden_norm = (hidden * rms_scale(hidden) * resid_gain[None, :]).astype(jnp.bfloat16)
    x_pre = jnp.dot(hidden_norm, w_in_x, preferred_element_type=jnp.float32).astype(jnp.bfloat16)
    bc_pre = jnp.dot(hidden_norm, w_in_bc, preferred_element_type=jnp.float32).astype(jnp.bfloat16)
    step_two = jax.nn.softplus(jnp.dot(hidden_norm, w_in_dt, preferred_element_type=jnp.float32) + step_time_bias[None, :])
    conv_taps = conv_x.shape[0]
    x_padded = jnp.concatenate([jnp.zeros((conv_taps - 1, x_pre.shape[1]), jnp.bfloat16), x_pre], axis=0)
    bc_padded = jnp.concatenate([jnp.zeros((conv_taps - 1, bc_pre.shape[1]), jnp.bfloat16), bc_pre], axis=0)
    x_two = jax.nn.silu(causal_conv(x_padded, conv_x, token_count)).astype(jnp.bfloat16)
    bc_two = jax.nn.silu(causal_conv(bc_padded, conv_bc, token_count)).astype(jnp.bfloat16)
    decay_two = log_decay(decay_code[1], decay_rate[1])
    mixed_two = ssd_layer(x_two, bc_two, step_two, decay_two, skip_gain[1])
    mixer_out = (mixed_two * rms_scale(mixed_two)).astype(jnp.bfloat16)
    return (resid_out, mixer_out)
```

```python
import functools

import jax
import jax.numpy as jnp
from jax import lax
from jax.experimental import pallas as pl
from jax.experimental.pallas import tpu as pltpu
from jax.sharding import PartitionSpec as P

CH = 64
GROUP = 256
F32 = jnp.float32
BF16 = jnp.bfloat16
NT = (((1,), (1,)), ((), ()))
VMEM = pl.BlockSpec(memory_space=pltpu.VMEM)
HALO = 16


def iota(shape, dim):
    return lax.broadcasted_iota(jnp.int32, shape, dim)


def exact_dot(a, b, dims=None):
    if dims is None:
        return jnp.dot(a, b, precision=lax.Precision.HIGHEST, preferred_element_type=F32)
    return lax.dot_general(a, b, dims, precision=lax.Precision.HIGHEST, preferred_element_type=F32)


def bdot(a, b, dims=None):
    if dims is None:
        return jnp.dot(a, b, preferred_element_type=F32)
    return lax.dot_general(a, b, dims, preferred_element_type=F32)


def split_two(v):
    hi = v.astype(BF16)
    return hi, (v - hi.astype(F32)).astype(BF16)


def spread(v, heads):
    width = heads * CH
    e = (iota((heads, width), 1) // CH == iota((heads, width), 0)).astype(BF16)
    hi, lo = split_two(v)
    return bdot(hi, e) + bdot(lo, e)


def lower(n):
    return iota((n, n), 0) >= iota((n, n), 1)


def states_body(x_ref, bc_ref, step_ref, code_ref, rate_ref, send_ref, st_ref, cum_ref):
    rows, heads = step_ref.shape
    blocks = rows // GROUP
    tri = lower(GROUP).astype(F32)
    totals = []
    state = None
    for b in range(blocks):
        r = pl.ds(b * GROUP, GROUP)
        decay = -jnp.minimum(code_ref[r, :].astype(F32) * rate_ref[...], 20.0)
        cum = exact_dot(tri, decay)
        cum_ref[r, :] = cum
        last = cum[GROUP - 1 : GROUP, :]
        weight = jnp.exp(last - cum) * step_ref[r, :]
        v = (x_ref[r, :].astype(F32) * spread(weight, heads)).astype(BF16)
        term = lax.dot_general(
            bc_ref[r, : bc_ref.shape[1] // 2], v, (((0,), (0,)), ((), ())), preferred_element_type=F32
        )
        if state is None:
            state = term
            st_ref[...] = term
        else:
            factor = spread(jnp.broadcast_to(jnp.exp(last), (8, heads)), heads)[0:1]
            state = factor * state + term
        totals.append(last)
    half = state.shape[0] // 2
    width = state.shape[1]
    send_ref[:, :width] = state[:half].astype(BF16)
    send_ref[:, width : 2 * width] = state[half:].astype(BF16)
    total = sum(totals[1:], totals[0])
    pieces = []
    rest = total
    for _ in range(3):
        piece = rest.astype(BF16).astype(F32)
        pieces.append(piece)
        rest = rest - piece
    pieces.append(jnp.zeros((1, 128 - 3 * heads), F32))
    tail = jnp.concatenate(pieces, axis=1)
    send_ref[:, 2 * width :] = jnp.broadcast_to(tail, (half, 128)).astype(BF16)


def scan_body(heads, got_ref, out_ref, s_ref, d_ref, p_ref):
    count = got_ref.shape[0]
    width = heads * CH
    s_ref[...] = got_ref[:, : 2 * width].astype(F32)
    tail = got_ref[:, 2 * width :].astype(F32)
    total = tail[:, :heads] + tail[:, heads : 2 * heads] + tail[:, 2 * heads : 3 * heads]
    d = spread(jnp.exp(total), heads)
    d_ref[:, :width] = d
    d_ref[:, width:] = d

    def one(k, p):
        row = pl.ds(k, 1)
        p_ref[row, :] = p
        return d_ref[row, :] * p + s_ref[row, :]

    lax.fori_loop(0, count, one, jnp.zeros((1, 2 * width), F32))
    out_ref[...] = p_ref[...].astype(BF16)


def diag_body(x_ref, bc_ref, step_ref, cum_ref, skip_ref, y_ref):
    rows, heads = step_ref.shape
    n = bc_ref.shape[1] // 2
    half = GROUP // 2
    eye = (iota((heads, heads), 0) == iota((heads, heads), 1)).astype(F32)
    left = iota((GROUP, 2 * CH), 1) < CH
    skip = spread(jnp.broadcast_to(skip_ref[...], (8, heads)), heads)[0:1]
    zero = jnp.zeros((), BF16)
    for b in range(rows // GROUP):
        r = pl.ds(b * GROUP, GROUP)
        scores = bdot(bc_ref[r, n:], bc_ref[r, :n], NT)
        scores = jnp.where(lower(GROUP), scores, 0.0)
        cum = cum_ref[r, :]
        cum_row = exact_dot(eye, cum, NT)
        step_row = exact_dot(eye, step_ref[r, :], NT)
        for pair in range(heads // 2):
            lanes = pl.ds(pair * 2 * CH, 2 * CH)
            xp = x_ref[r, lanes]
            tops, bottoms = [], []
            for side in range(2):
                h = 2 * pair + side
                mine = jnp.where(left if side == 0 else ~left, xp, zero)
                col = cum[:, h : h + 1]
                row = cum_row[h : h + 1, :]
                srow = step_row[h : h + 1, :]
                top = (
                    jnp.exp(jnp.minimum(col[:half] - row[:, :half], 0.0))
                    * scores[:half, :half]
                    * srow[:, :half]
                ).astype(BF16)
                bottom = (
                    jnp.exp(jnp.minimum(col[half:] - row, 0.0)) * scores[half:, :] * srow
                ).astype(BF16)
                tops.append(bdot(top, mine[:half]))
                bottoms.append(bdot(bottom, mine))
            xs = xp.astype(F32) * skip[:, pair * 2 * CH : (pair + 1) * 2 * CH]
            y_ref[pl.ds(b * GROUP, half), lanes] = tops[0] + tops[1] + xs[:half]
            y_ref[pl.ds(b * GROUP + half, half), lanes] = bottoms[0] + bottoms[1] + xs[half:]


def mixed_blocks(bc_ref, cum_ref, prev_ref, st_ref, y_ref):
    rows, heads = cum_ref.shape
    width = heads * CH
    n = bc_ref.shape[1] // 2
    out = []
    low = high = None
    for b in range(rows // GROUP):
        r = pl.ds(b * GROUP, GROUP)
        c = bc_ref[r, n:]
        cum = cum_ref[r, :]
        if b == 0:
            high = jnp.concatenate([prev_ref[:, :width], prev_ref[:, width:]], axis=0)
            inner = bdot(c, high)
        else:
            last = cum_ref[pl.ds(GROUP - 8, 8), :]
            factor = spread(jnp.exp(last), heads)[7:8]
            state = factor * high.astype(F32) + st_ref[...]
            hi, lo = split_two(state)
            inner = bdot(c, hi) + bdot(c, lo)
        out.append((r, y_ref[r, :] + inner * spread(jnp.exp(cum), heads)))
    return out


def gate_body(bc_ref, cum_ref, prev_ref, st_ref, y_ref, gate_ref, gain_ref, g_ref, ss_ref):
    ones = jnp.ones((8, g_ref.shape[1]), F32)
    for r, mixed in mixed_blocks(bc_ref, cum_ref, prev_ref, st_ref, y_ref):
        gate = gate_ref[r, :].astype(F32)
        gated = mixed * (gate / (1.0 + jnp.exp(-gate)))
        g_ref[r, :] = (gated * gain_ref[...]).astype(BF16)
        ss_ref[:, r] = exact_dot(ones, gated * gated, NT)


def last_body(bc_ref, cum_ref, prev_ref, st_ref, y_ref, m_ref, ss_ref):
    ones = jnp.ones((8, m_ref.shape[1]), F32)
    for r, mixed in mixed_blocks(bc_ref, cum_ref, prev_ref, st_ref, y_ref):
        m_ref[r, :] = mixed
        ss_ref[:, r] = exact_dot(ones, mixed * mixed, NT)


def second_body(
    hid_ref, halo_ref, gain_ref, w_ref, bias_ref, cx_ref, cbc_ref, x_ref, bc_ref, step_ref, h_ref, pre_ref, rs_ref
):
    rows, depth = hid_ref.shape
    width = x_ref.shape[1]
    heads = step_ref.shape[1]
    states = bc_ref.shape[1]
    first = lax.axis_index("seq") == 0

    def scaled(src, r, at, n, keep):
        v = src[r, :].astype(F32)
        rs = lax.rsqrt(jnp.sum(v * v, axis=1, keepdims=True) / depth + 1e-05)
        rs_ref[pl.ds(at, n), :] = jnp.broadcast_to(rs if keep is None else rs * keep, (n, 128))
        h_ref[pl.ds(at, n), :] = (v * gain_ref[...]).astype(BF16)

    scaled(halo_ref, pl.ds(0, HALO), 0, HALO, jnp.where(first, 0.0, 1.0))
    step = 64

    @pl.loop(0, rows // step)
    def _(i):
        at = pl.multiple_of(i * step, step)
        scaled(hid_ref, pl.ds(at, step), pl.multiple_of(at + HALO, 16), step, None)

    def project(cols):
        return bdot(h_ref[...], w_ref[:, cols])

    def conv(taps, k):
        n = taps.shape[1]
        total = None
        for tap in range(k):
            v = pre_ref[pl.ds(HALO - k + 1 + tap, rows), :n] * taps[tap : tap + 1, :].astype(F32)
            total = v if total is None else total + v
        return (total / (1.0 + jnp.exp(-total))).astype(BF16)

    tile = 256
    rs_all = rs_ref[...]
    rs2 = jnp.concatenate([rs_all, rs_all], axis=1)

    @pl.loop(0, width // tile)
    def _(i):
        at = pl.multiple_of(i * tile, tile)
        cols = pl.ds(at, tile)
        pre_ref[...] = (project(cols) * rs2).astype(BF16).astype(F32)
        x_ref[:, cols] = conv(cx_ref[:, cols], cx_ref.shape[0])

    pre_ref[...] = (project(pl.ds(width, states)) * rs2).astype(BF16).astype(F32)
    bc_ref[...] = conv(cbc_ref[...], cbc_ref.shape[0])
    dt = bdot(h_ref[pl.ds(HALO, rows), :], w_ref[:, pl.ds(width + states, 128)])
    dt = (dt * rs_ref[pl.ds(HALO, rows), :])[:, :heads] + bias_ref[...]
    step_ref[...] = jnp.maximum(dt, 0.0) + jnp.log(1.0 + jnp.exp(-jnp.abs(dt)))


def call(body, outs, args, scratch=(), limit=56, **kw):
    return pl.pallas_call(
        body,
        out_shape=outs,
        in_specs=[VMEM] * len(args),
        out_specs=jax.tree.map(lambda _: VMEM, outs),
        scratch_shapes=list(scratch),
        compiler_params=pltpu.CompilerParams(vmem_limit_bytes=limit * 2**20, **kw),
    )(*args)


def sds(*shape, dtype=F32):
    return jax.ShapeDtypeStruct(shape, dtype)


def prefix(send, heads):
    count, wide = send.shape
    got = lax.all_to_all(send, "seq", 0, 0, tiled=True)
    width = wide - 128
    back = call(
        functools.partial(scan_body, heads),
        sds(count, width, dtype=BF16),
        (got,),
        [pltpu.VMEM((count, width), F32) for _ in range(3)],
    )
    return lax.all_to_all(back, "seq", 0, 0, tiled=True)


def local_states(x, bc, step, code, rate):
    rows, heads = step.shape
    n = bc.shape[1] // 2
    width = heads * CH
    return call(
        states_body,
        (sds(n // 2, 2 * width + 128, dtype=BF16), sds(n, width), sds(rows, heads)),
        (x, bc, step, code, rate),
    )


def diagonal(x, bc, step, cum, skip):
    return call(diag_body, sds(*x.shape), (x, bc, step, cum, skip))


def on_device(
    x_in, gate_in, bc_in, step_in, decay_code, decay_rate, skip_gain, norm_gain, w_out, resid_in,
    resid_gain, w_in_x, w_in_bc, w_in_dt, step_time_bias, conv_x, conv_bc,
):
    rows, width = x_in.shape
    heads = step_in.shape[1]
    inner = width * lax.axis_size("head")
    w_out_all = lax.all_gather(w_out, "seq", axis=1, tiled=True)
    w_in = jnp.concatenate(
        [w_in_x, w_in_bc, jnp.pad(w_in_dt, ((0, 0), (0, 128 - heads)))], axis=1
    )
    w_in_all = lax.all_gather(w_in, "seq", axis=0, tiled=True)

    send, st, cum = local_states(x_in, bc_in, step_in, decay_code[0], decay_rate[0:1])
    y = diagonal(x_in, bc_in, step_in, cum, skip_gain[0:1])
    prev = prefix(send, heads)
    g, ss = call(
        gate_body,
        (sds(rows, width, dtype=BF16), sds(8, rows)),
        (bc_in, cum, prev, st, y, gate_in, norm_gain[None, :]),
    )
    rs = lax.rsqrt(lax.psum(ss[0], "head") / inner + 1e-05)
    projected = jnp.dot(g, w_out_all, preferred_element_type=F32).astype(BF16)
    share = lax.psum_scatter(projected, "head", scatter_dimension=1, tiled=True)
    resid_out = (resid_in.astype(F32) + share.astype(F32) * rs[:, None]).astype(BF16)
    hidden = lax.all_gather(resid_out, "head", axis=1, tiled=True)
    size = lax.axis_size("seq")
    halo = lax.ppermute(hidden[rows - HALO :], "seq", [(i, i + 1) for i in range(size - 1)])

    x_two, bc_two, step_two = call(
        second_body,
        (sds(rows, width, dtype=BF16), sds(*bc_in.shape, dtype=BF16), sds(rows, heads)),
        (hidden, halo, resid_gain[None, :], w_in_all, step_time_bias[None, :], conv_x, conv_bc),
        [
            pltpu.VMEM((rows + HALO, inner), BF16),
            pltpu.VMEM((rows + HALO, 256), F32),
            pltpu.VMEM((rows + HALO, 128), F32),
        ],
    )
    send, st, cum = local_states(x_two, bc_two, step_two, decay_code[1], decay_rate[1:2])
    y = diagonal(x_two, bc_two, step_two, cum, skip_gain[1:2])
    prev = prefix(send, heads)
    mixed, ss = call(last_body, (sds(rows, width), sds(8, rows)), (bc_two, cum, prev, st, y))
    rs = lax.rsqrt(lax.psum(ss[0], "head") / inner + 1e-05)
    return resid_out, (mixed * rs[:, None]).astype(BF16)


def solution(mesh):
    in_specs = (
        P("seq", "head"), P("seq", "head"), P("seq", None), P("seq", "head"), P(None, "seq", "head"),
        P(None, "head"), P(None, "head"), P("head"), P("head", "seq"), P("seq", "head"), P(),
        P("seq", "head"), P("seq", None), P("seq", "head"), P("head"), P(None, "head"), P(),
    )
    out_specs = (P("seq", "head"), P("seq", "head"))
    return jax.shard_map(
        on_device, mesh=mesh, in_specs=in_specs, out_specs=out_specs, check_vma=False
    )
```

```python
import functools

import jax
import jax.numpy as jnp
from jax import lax
from jax.experimental import pallas as pl
from jax.experimental.pallas import tpu as pltpu
from jax.sharding import PartitionSpec as P

CH = 64
GROUP = 256
F32 = jnp.float32
BF16 = jnp.bfloat16
NT = (((1,), (1,)), ((), ()))
VMEM = pl.BlockSpec(memory_space=pltpu.VMEM)
HALO = 16


def iota(shape, dim):
    return lax.broadcasted_iota(jnp.int32, shape, dim)


def exact_dot(a, b, dims=None):
    if dims is None:
        return jnp.dot(a, b, precision=lax.Precision.HIGHEST, preferred_element_type=F32)
    return lax.dot_general(a, b, dims, precision=lax.Precision.HIGHEST, preferred_element_type=F32)


def bdot(a, b, dims=None):
    if dims is None:
        return jnp.dot(a, b, preferred_element_type=F32)
    return lax.dot_general(a, b, dims, preferred_element_type=F32)


def split_two(v):
    hi = v.astype(BF16)
    return hi, (v - hi.astype(F32)).astype(BF16)


def spread(v, heads):
    width = heads * CH
    e = (iota((heads, width), 1) // CH == iota((heads, width), 0)).astype(BF16)
    hi, lo = split_two(v)
    return bdot(hi, e) + bdot(lo, e)


def lower(n):
    return iota((n, n), 0) >= iota((n, n), 1)


def states_body(x_ref, bc_ref, step_ref, code_ref, rate_ref, send_ref, st_ref, cum_ref):
    rows, heads = step_ref.shape
    blocks = rows // GROUP
    tri = lower(GROUP).astype(F32)
    totals = []
    state = None
    for b in range(blocks):
        r = pl.ds(b * GROUP, GROUP)
        decay = -jnp.minimum(code_ref[r, :].astype(F32) * rate_ref[...], 20.0)
        cum = exact_dot(tri, decay)
        cum_ref[r, :] = cum
        last = cum[GROUP - 1 : GROUP, :]
        weight = jnp.exp(last - cum) * step_ref[r, :]
        v = (x_ref[r, :].astype(F32) * spread(weight, heads)).astype(BF16)
        term = lax.dot_general(
            bc_ref[r, : bc_ref.shape[1] // 2], v, (((0,), (0,)), ((), ())), preferred_element_type=F32
        )
        if state is None:
            state = term
            st_ref[...] = term
        else:
            factor = spread(jnp.broadcast_to(jnp.exp(last), (8, heads)), heads)[0:1]
            state = factor * state + term
        totals.append(last)
    half = state.shape[0] // 2
    width = state.shape[1]
    send_ref[:, :width] = state[:half].astype(BF16)
    send_ref[:, width : 2 * width] = state[half:].astype(BF16)
    total = sum(totals[1:], totals[0])
    pieces = []
    rest = total
    for _ in range(3):
        piece = rest.astype(BF16).astype(F32)
        pieces.append(piece)
        rest = rest - piece
    pieces.append(jnp.zeros((1, 128 - 3 * heads), F32))
    tail = jnp.concatenate(pieces, axis=1)
    send_ref[:, 2 * width :] = jnp.broadcast_to(tail, (half, 128)).astype(BF16)


def scan_body(heads, got_ref, out_ref, s_ref, d_ref, p_ref):
    count = got_ref.shape[0]
    width = heads * CH
    s_ref[...] = got_ref[:, : 2 * width].astype(F32)
    tail = got_ref[:, 2 * width :].astype(F32)
    total = tail[:, :heads] + tail[:, heads : 2 * heads] + tail[:, 2 * heads : 3 * heads]
    d = spread(jnp.exp(total), heads)
    d_ref[:, :width] = d
    d_ref[:, width:] = d

    def one(k, p):
        row = pl.ds(k, 1)
        p_ref[row, :] = p
        return d_ref[row, :] * p + s_ref[row, :]

    lax.fori_loop(0, count, one, jnp.zeros((1, 2 * width), F32))
    out_ref[...] = p_ref[...].astype(BF16)


def diag_body(x_ref, bc_ref, step_ref, cum_ref, skip_ref, y_ref):
    rows, heads = step_ref.shape
    n = bc_ref.shape[1] // 2
    half = GROUP // 2
    eye = (iota((heads, heads), 0) == iota((heads, heads), 1)).astype(F32)
    left = iota((GROUP, 2 * CH), 1) < CH
    skip = spread(jnp.broadcast_to(skip_ref[...], (8, heads)), heads)[0:1]
    zero = jnp.zeros((), BF16)
    for b in range(rows // GROUP):
        r = pl.ds(b * GROUP, GROUP)
        scores = bdot(bc_ref[r, n:], bc_ref[r, :n], NT)
        scores = jnp.where(lower(GROUP), scores, 0.0)
        cum = cum_ref[r, :]
        cum_row = exact_dot(eye, cum, NT)
        step_row = exact_dot(eye, step_ref[r, :], NT)
        for pair in range(heads // 2):
            lanes = pl.ds(pair * 2 * CH, 2 * CH)
            xp = x_ref[r, lanes]
            tops, bottoms = [], []
            for side in range(2):
                h = 2 * pair + side
                mine = jnp.where(left if side == 0 else ~left, xp, zero)
                col = cum[:, h : h + 1]
                row = cum_row[h : h + 1, :]
                srow = step_row[h : h + 1, :]
                top = (
                    jnp.exp(jnp.minimum(col[:half] - row[:, :half], 0.0))
                    * scores[:half, :half]
                    * srow[:, :half]
                ).astype(BF16)
                bottom = (
                    jnp.exp(jnp.minimum(col[half:] - row, 0.0)) * scores[half:, :] * srow
                ).astype(BF16)
                tops.append(bdot(top, mine[:half]))
                bottoms.append(bdot(bottom, mine))
            xs = xp.astype(F32) * skip[:, pair * 2 * CH : (pair + 1) * 2 * CH]
            y_ref[pl.ds(b * GROUP, half), lanes] = tops[0] + tops[1] + xs[:half]
            y_ref[pl.ds(b * GROUP + half, half), lanes] = bottoms[0] + bottoms[1] + xs[half:]


def mixed_blocks(bc_ref, cum_ref, prev_ref, st_ref, y_ref):
    rows, heads = cum_ref.shape
    width = heads * CH
    n = bc_ref.shape[1] // 2
    out = []
    low = high = None
    for b in range(rows // GROUP):
        r = pl.ds(b * GROUP, GROUP)
        c = bc_ref[r, n:]
        cum = cum_ref[r, :]
        if b == 0:
            high = jnp.concatenate([prev_ref[:, :width], prev_ref[:, width:]], axis=0)
            inner = bdot(c, high)
        else:
            last = cum_ref[pl.ds(GROUP - 8, 8), :]
            factor = spread(jnp.exp(last), heads)[7:8]
            state = factor * high.astype(F32) + st_ref[...]
            hi, lo = split_two(state)
            inner = bdot(c, hi) + bdot(c, lo)
        out.append((r, y_ref[r, :] + inner * spread(jnp.exp(cum), heads)))
    return out


def gate_body(bc_ref, cum_ref, prev_ref, st_ref, y_ref, gate_ref, gain_ref, g_ref, ss_ref):
    ones = jnp.ones((8, g_ref.shape[1]), F32)
    for r, mixed in mixed_blocks(bc_ref, cum_ref, prev_ref, st_ref, y_ref):
        gate = gate_ref[r, :].astype(F32)
        gated = mixed * (gate / (1.0 + jnp.exp(-gate)))
        g_ref[r, :] = (gated * gain_ref[...]).astype(BF16)
        ss_ref[:, r] = exact_dot(ones, gated * gated, NT)


def last_body(bc_ref, cum_ref, prev_ref, st_ref, y_ref, m_ref, ss_ref):
    ones = jnp.ones((8, m_ref.shape[1]), F32)
    for r, mixed in mixed_blocks(bc_ref, cum_ref, prev_ref, st_ref, y_ref):
        m_ref[r, :] = mixed
        ss_ref[:, r] = exact_dot(ones, mixed * mixed, NT)


NC = 8
CHUNK_LAG = 2
MESH = pl.DeviceIdType.MESH
Y, Z, CORES = 4, 8, 2


def place():
    seq = lax.axis_index("seq")
    return seq // (Z * CORES), (seq // CORES) % Z, seq % CORES


def seq_of(y, z, c):
    return (y * Z + z) * CORES + c


class Copies:
    def __init__(self, send_sem, recv_sem):
        self.send_sem, self.recv_sem = send_sem, recv_sem
        self.names = {}
        self.started = []

    def _make(self, name, src, dst, device):
        at = self.names.setdefault(name, len(self.names))
        return pltpu.make_async_remote_copy(
            src_ref=src, dst_ref=dst, send_sem=self.send_sem.at[at], recv_sem=self.recv_sem.at[at],
            device_id=device, device_id_type=MESH,
        )

    def send(self, name, src, dst, device):
        copy = self._make(name, src, dst, device)
        copy.start()
        self.started.append(copy)

    def arrived(self, name, where, device):
        self._make(name, where, where, device).wait_recv()

    def finish(self):
        for copy in self.started:
            copy.wait_send()


def weight_steps(cp, own, w, local_sem):
    y, z, c = place()
    head = lax.axis_index("head")
    half = own.shape[0] // 2
    f = 1 - 2 * c
    top, low = pl.ds(0, half), pl.ds(half, half)

    def at_y(k):
        return lax.rem(y + k * f + 2 * Y, Y)

    def at_z(k):
        return lax.rem(z + k * f + 2 * Z, Z)

    to_y = {k: (seq_of(at_y(k), z, c), head) for k in (1, -1)}
    to_z = {k: (seq_of(y, at_z(k), c), head) for k in (1, -1)}
    other = (seq_of(y, z, 1 - c), head)

    def a_piece(ky):
        return w.at[at_y(ky), z, c, top]

    def a_block(kz):
        return w.at[:, at_z(kz), c, top]

    def b_piece(kz):
        return w.at[y, at_z(kz), c, low]

    def b_block(ky):
        return w.at[at_y(ky), :, c, low]

    def push(name, ref, device):
        cp.send(name, ref, ref, device)

    def a_share(kz):
        push(("as", kz), a_block(kz), other)

    def b_share(ky):
        push(("bs", ky), b_block(ky), other)

    def a_went(way, k):
        cp.arrived(("az", way, k), a_block(-way * (k + 1)), to_z[way])
        if k < (3 if way == 1 else 2):
            push(("az", way, k + 1), a_block(-way * (k + 1)), to_z[way])
        a_share(-way * (k + 1))

    def b_went(way, k):
        cp.arrived(("bz", way, k), b_piece(-way * (k + 1)), to_z[way])
        if k < (3 if way == -1 else 2):
            push(("bz", way, k + 1), b_piece(-way * (k + 1)), to_z[way])

    def s0():
        mine = pltpu.make_async_copy(own, w.at[y, z, c], local_sem)
        mine.start()
        for way in (1, -1):
            cp.send(("ay", way, 0), own.at[top], a_piece(0), to_y[way])
            cp.send(("bz", way, 0), own.at[low], b_piece(0), to_z[way])
        mine.wait()

    def s1():
        cp.arrived(("ay", 1, 0), a_piece(-1), to_y[1])
        push(("ay", 1, 1), a_piece(-1), to_y[1])
        b_went(1, 0)
        b_went(-1, 0)

    def s2():
        cp.arrived(("ay", -1, 0), a_piece(1), to_y[-1])
        cp.arrived(("ay", 1, 1), a_piece(-2), to_y[1])
        for way in (1, -1):
            push(("az", way, 0), a_block(0), to_z[way])
        a_share(0)
        b_went(1, 1)
        b_went(-1, 1)

    def s3():
        b_went(1, 2)
        b_went(-1, 2)
        a_went(1, 0)
        a_went(-1, 0)

    def s4():
        b_went(-1, 3)
        for way in (1, -1):
            push(("by", way, 0), b_block(0), to_y[way])
        b_share(0)
        a_went(1, 1)
        a_went(-1, 1)

    def s5():
        a_went(1, 2)
        a_went(-1, 2)
        cp.arrived(("by", -1, 0), b_block(1), to_y[-1])
        push(("by", -1, 1), b_block(1), to_y[-1])
        b_share(1)
        cp.arrived(("by", 1, 0), b_block(-1), to_y[1])
        b_share(-1)

    def s6():
        a_went(1, 3)
        cp.arrived(("by", -1, 1), b_block(2), to_y[-1])
        b_share(2)

    def s7():
        for kz in range(-4, 4):
            where = w.at[:, lax.rem(z - kz * f + 2 * Z, Z), 1 - c, top]
            cp.arrived(("as", kz), where, other)
        for ky in range(-1, 3):
            where = w.at[lax.rem(y - ky * f + 2 * Y, Y), :, 1 - c, low]
            cp.arrived(("bs", ky), where, other)

    return [s0, s1, s2, s3, s4, s5, s6, s7], [*to_y.values(), *to_z.values(), other]


N_WEIGHT_COPIES = 32


def greet(devices):
    barrier = pltpu.get_barrier_semaphore()
    for device in devices:
        pl.semaphore_signal(barrier, inc=1, device_id=device, device_id_type=MESH)
    pl.semaphore_wait(barrier, len(devices))


def handoff_body(
    g_ref, ss_ref, wo_ref, resid_ref, wi_ref, gain_ref, bias_ref, cx_ref, cbc_ref,
    out_ref, x_ref, bc_ref, step_ref,
    w_ref, hid_ref, h_ref, opp_ref, right_ref, left_ref, own_ref, sum_r_ref, sum_l_ref,
    in_l1, in_r1, in_l2, in_r2, ss_in, tail_ref, halo_ref, scale_ref, rs_ref, pre_ref,
    send_sem, recv_sem, local_sem,
):
    rows, width = g_ref.shape
    heads = step_ref.shape[1]
    states = bc_ref.shape[1]
    seq, me = lax.axis_index("seq"), lax.axis_index("head")
    n_seq, n_head = lax.axis_size("seq"), lax.axis_size("head")
    depth = width * n_head
    r, o, l = (lax.rem(me + k, n_head) for k in (1, 2, 3))
    right, opposite, left = ((seq, k) for k in (r, o, l))
    after, before = ((lax.rem(seq + k, n_seq), me) for k in (1, n_seq - 1))
    cp = Copies(send_sem, recv_sem)
    steps, partners = weight_steps(cp, wi_ref, w_ref, local_sem)
    greet([right, left, opposite, after, before, *partners])
    chunk = rows // NC
    half = width // 2
    lo, hi = pl.ds(0, half), pl.ds(half, half)
    order = [NC - 1 - k for k in range(NC)]
    tile = 256

    def cut(c):
        return pl.ds(c * chunk, chunk)

    steps.pop(0)()
    for k, device in ((1, right), (2, opposite), (3, left)):
        cp.send(("ss", k), ss_ref, ss_in.at[k - 1], device)

    def product(first, n, dest, store):
        @pl.loop(0, width // tile)
        def _(j):
            at = pl.multiple_of(j * tile, tile)
            cols = pl.ds(pl.multiple_of(dest * width + at, tile), tile)
            store(pl.ds(at, tile), bdot(g_ref[pl.ds(first, n), :], wo_ref[:, cols]))

    def project(k):
        if k % 2:
            return
        first, n = order[k + 1] * chunk, 2 * chunk
        at = pl.ds(first, n)

        def to_opp(cols, p):
            opp_ref[at, cols] = p.astype(BF16)

        def keep(ref):
            def store(cols, p):
                ref[at, cols] = p

            return store

        product(first, n, o, to_opp)
        for c in (order[k], order[k + 1]):
            cp.send(("1r", c), opp_ref.at[cut(c), lo], in_l1.at[cut(c)], right)
            cp.send(("1l", c), opp_ref.at[cut(c), hi], in_r1.at[cut(c)], left)
        product(first, n, r, keep(right_ref))
        product(first, n, l, keep(left_ref))
        product(first, n, me, keep(own_ref))

    def second_sum(c):
        q = cut(c)
        cp.arrived(("1r", c), in_l1.at[q], right)
        sum_r_ref[q, lo] = (right_ref[q, lo] + in_l1[q, :].astype(F32)).astype(BF16)
        sum_r_ref[q, hi] = right_ref[q, hi].astype(BF16)
        cp.send(("2r", c), sum_r_ref.at[q], in_l2.at[q], right)
        cp.arrived(("1l", c), in_r1.at[q], left)
        sum_l_ref[q, hi] = (left_ref[q, hi] + in_r1[q, :].astype(F32)).astype(BF16)
        sum_l_ref[q, lo] = left_ref[q, lo].astype(BF16)
        cp.send(("2l", c), sum_l_ref.at[q], in_r2.at[q], left)

    def token_scale():
        for k, device in ((1, right), (2, opposite), (3, left)):
            cp.arrived(("ss", k), ss_in.at[k - 1], device)
        total = ss_ref[...] + ss_in[0] + ss_in[1] + ss_in[2]
        eighth = jnp.full((8, 128), 0.125, F32)
        column = exact_dot(total, eighth, (((0,), (0,)), ((), ())))
        scale_ref[...] = lax.rsqrt(column / depth + 1e-05)

    def residual(c):
        q = cut(c)
        cp.arrived(("2r", c), in_l2.at[q], right)
        cp.arrived(("2l", c), in_r2.at[q], left)
        total = own_ref[q, :] + in_l2[q, :].astype(F32) + in_r2[q, :].astype(F32)
        total = total * scale_ref[q, 0:1] + resid_ref[q, :].astype(F32)
        out_ref[q, :] = total.astype(BF16)
        hid_ref[me, q, :] = out_ref[q, :]
        cp.send(("3r", c), hid_ref.at[me, q], hid_ref.at[me, q], right)
        cp.send(("3l", c), hid_ref.at[me, q], hid_ref.at[me, q], left)

    def hand_on(c):
        q = cut(c)
        cp.arrived(("3r", c), hid_ref.at[l, q], right)
        cp.send(("4r", c), hid_ref.at[l, q, lo], hid_ref.at[l, q, lo], right)
        cp.arrived(("3l", c), hid_ref.at[r, q], left)
        cp.send(("4l", c), hid_ref.at[r, q, hi], hid_ref.at[r, q, hi], left)

    def scaled(src, q, at, n, keep):
        parts = [src[k, q, :].astype(F32) for k in range(n_head)]
        total = sum(jnp.sum(v * v, axis=1, keepdims=True) for v in parts)
        rs = lax.rsqrt(total / depth + 1e-05)
        rs_ref[pl.ds(at, n), :] = jnp.broadcast_to(rs if keep is None else rs * keep, (n, 128))
        for k, v in enumerate(parts):
            h_ref[k, pl.ds(at, n), :] = (v * gain_ref[:, k * width : (k + 1) * width]).astype(BF16)

    def complete(c):
        q = cut(c)
        cp.arrived(("4r", c), hid_ref.at[o, q, lo], right)
        cp.arrived(("4l", c), hid_ref.at[o, q, hi], left)
        if c == NC - 1:
            tail_ref[...] = hid_ref[:, pl.ds(rows - HALO, HALO), :]
            cp.send("halo", tail_ref, halo_ref, after)
        scaled(hid_ref, q, c * chunk + HALO, chunk, None)

    for t in range(NC + 4 * CHUNK_LAG):
        for stage, work in reversed(list(enumerate((project, second_sum, residual, hand_on, complete)))):
            k = t - CHUNK_LAG * stage
            if 0 <= k < NC:
                if work is residual and k == 0:
                    token_scale()
                work(k if work is project else order[k])
        if steps:
            steps.pop(0)()
    while steps:
        steps.pop(0)()
    cp.arrived("halo", halo_ref, after)
    scaled(halo_ref, pl.ds(0, HALO), 0, HALO, jnp.where(seq == 0, 0.0, 1.0))

    def into(cols, at, n):
        total = None
        for k in range(n_head):
            piece = bdot(
                h_ref[k, pl.ds(at, n), :], w_ref[k, :, :, :, cols].reshape(width, cols.size)
            )
            total = piece if total is None else total + piece
        return total

    def conv(taps, k):
        n = taps.shape[1]
        total = None
        for tap in range(k):
            v = pre_ref[pl.ds(HALO - k + 1 + tap, rows), :n] * taps[tap : tap + 1, :].astype(F32)
            total = v if total is None else total + v
        return (total / (1.0 + jnp.exp(-total))).astype(BF16)

    every = rows + HALO

    def pre(cols):
        rs = rs_ref[...]
        pre_ref[...] = (into(cols, 0, every) * jnp.concatenate([rs, rs], axis=1)).astype(BF16).astype(F32)

    @pl.loop(0, width // tile)
    def _(i):
        cols = pl.ds(pl.multiple_of(i * tile, tile), tile)
        pre(cols)
        x_ref[:, cols] = conv(cx_ref[:, cols], cx_ref.shape[0])

    pre(pl.ds(width, states))
    bc_ref[...] = conv(cbc_ref[...], cbc_ref.shape[0])
    dt = into(pl.ds(width + states, 128), HALO, rows)
    dt = (dt * rs_ref[pl.ds(HALO, rows), :])[:, :heads] + bias_ref[...]
    step_ref[...] = jnp.maximum(dt, 0.0) + jnp.log(1.0 + jnp.exp(-jnp.abs(dt)))
    cp.finish()


def handoff(g, ss, w_out_all, resid, w_in, gain, bias, conv_x, conv_bc, heads):
    rows, width = g.shape
    n_head = lax.axis_size("head")
    states = conv_bc.shape[1]
    copies = N_WEIGHT_COPIES + 3 + 1 + 8 * NC
    return call(
        handoff_body,
        (
            sds(rows, width, dtype=BF16), sds(rows, width, dtype=BF16),
            sds(rows, states, dtype=BF16), sds(rows, heads),
        ),
        (g, ss, w_out_all, resid, w_in, gain, bias, conv_x, conv_bc),
        [
            pltpu.VMEM((Y, Z, CORES, *w_in.shape), BF16),
            pltpu.VMEM((n_head, rows, width), BF16),
            pltpu.VMEM((n_head, rows + HALO, width), BF16),
            pltpu.VMEM((rows, width), BF16),
            *[pltpu.VMEM((rows, width), F32) for _ in range(3)],
            *[pltpu.VMEM((rows, width), BF16) for _ in range(2)],
            *[pltpu.VMEM((rows, width // 2), BF16) for _ in range(2)],
            *[pltpu.VMEM((rows, width), BF16) for _ in range(2)],
            pltpu.VMEM((3, *ss.shape), F32),
            *[pltpu.VMEM((n_head, HALO, width), BF16) for _ in range(2)],
            pltpu.VMEM((rows, 128), F32),
            pltpu.VMEM((rows + HALO, 128), F32),
            pltpu.VMEM((rows + HALO, 256), F32),
            pltpu.SemaphoreType.DMA((copies,)),
            pltpu.SemaphoreType.DMA((copies,)),
            pltpu.SemaphoreType.DMA,
        ],
        limit=60,
        collective_id=1,
        has_side_effects=True,
    )


def call(body, outs, args, scratch=(), limit=56, **kw):
    return pl.pallas_call(
        body,
        out_shape=outs,
        in_specs=[VMEM] * len(args),
        out_specs=jax.tree.map(lambda _: VMEM, outs),
        scratch_shapes=list(scratch),
        compiler_params=pltpu.CompilerParams(vmem_limit_bytes=limit * 2**20, **kw),
    )(*args)


def sds(*shape, dtype=F32):
    return jax.ShapeDtypeStruct(shape, dtype)


def prefix(send, heads):
    count, wide = send.shape
    got = lax.all_to_all(send, "seq", 0, 0, tiled=True)
    width = wide - 128
    back = call(
        functools.partial(scan_body, heads),
        sds(count, width, dtype=BF16),
        (got,),
        [pltpu.VMEM((count, width), F32) for _ in range(3)],
    )
    return lax.all_to_all(back, "seq", 0, 0, tiled=True)


def local_states(x, bc, step, code, rate):
    rows, heads = step.shape
    n = bc.shape[1] // 2
    width = heads * CH
    return call(
        states_body,
        (sds(n // 2, 2 * width + 128, dtype=BF16), sds(n, width), sds(rows, heads)),
        (x, bc, step, code, rate),
    )


def diagonal(x, bc, step, cum, skip):
    return call(diag_body, sds(*x.shape), (x, bc, step, cum, skip))


def on_device(
    x_in, gate_in, bc_in, step_in, decay_code, decay_rate, skip_gain, norm_gain, w_out, resid_in,
    resid_gain, w_in_x, w_in_bc, w_in_dt, step_time_bias, conv_x, conv_bc,
):
    rows, width = x_in.shape
    heads = step_in.shape[1]
    inner = width * lax.axis_size("head")
    w_out_all = lax.all_gather(w_out, "seq", axis=1, tiled=True)
    w_in = jnp.concatenate(
        [w_in_x, w_in_bc, jnp.pad(w_in_dt, ((0, 0), (0, 128 - heads)))], axis=1
    )

    send, st, cum = local_states(x_in, bc_in, step_in, decay_code[0], decay_rate[0:1])
    y = diagonal(x_in, bc_in, step_in, cum, skip_gain[0:1])
    prev = prefix(send, heads)
    g, ss = call(
        gate_body,
        (sds(rows, width, dtype=BF16), sds(8, rows)),
        (bc_in, cum, prev, st, y, gate_in, norm_gain[None, :]),
    )
    resid_out, x_two, bc_two, step_two = handoff(
        g, ss, w_out_all, resid_in, w_in, resid_gain[None, :], step_time_bias[None, :], conv_x, conv_bc, heads
    )
    send, st, cum = local_states(x_two, bc_two, step_two, decay_code[1], decay_rate[1:2])
    y = diagonal(x_two, bc_two, step_two, cum, skip_gain[1:2])
    prev = prefix(send, heads)
    mixed, ss = call(last_body, (sds(rows, width), sds(8, rows)), (bc_two, cum, prev, st, y))
    rs = lax.rsqrt(lax.psum(ss[0], "head") / inner + 1e-05)
    return resid_out, (mixed * rs[:, None]).astype(BF16)


def solution(mesh):
    in_specs = (
        P("seq", "head"), P("seq", "head"), P("seq", None), P("seq", "head"), P(None, "seq", "head"),
        P(None, "head"), P(None, "head"), P("head"), P("head", "seq"), P("seq", "head"), P(),
        P("seq", "head"), P("seq", None), P("seq", "head"), P("head"), P(None, "head"), P(),
    )
    out_specs = (P("seq", "head"), P("seq", "head"))
    return jax.shard_map(
        on_device, mesh=mesh, in_specs=in_specs, out_specs=out_specs, check_vma=False
    )
```

```python
import functools
import types

import jax
import jax.numpy as jnp
from jax import lax
from jax.experimental import pallas as pl
from jax.experimental.pallas import tpu as pltpu
from jax.sharding import PartitionSpec as P

CH = 64
GROUP = 256
F32 = jnp.float32
BF16 = jnp.bfloat16
NT = (((1,), (1,)), ((), ()))
VMEM = pl.BlockSpec(memory_space=pltpu.VMEM)
HALO = 16


def iota(shape, dim):
    return lax.broadcasted_iota(jnp.int32, shape, dim)


def exact_dot(a, b, dims=None):
    if dims is None:
        return jnp.dot(a, b, precision=lax.Precision.HIGHEST, preferred_element_type=F32)
    return lax.dot_general(a, b, dims, precision=lax.Precision.HIGHEST, preferred_element_type=F32)


def bdot(a, b, dims=None):
    if dims is None:
        return jnp.dot(a, b, preferred_element_type=F32)
    return lax.dot_general(a, b, dims, preferred_element_type=F32)


def split_two(v):
    hi = v.astype(BF16)
    return hi, (v - hi.astype(F32)).astype(BF16)


def spread(v, heads):
    width = heads * CH
    e = (iota((heads, width), 1) // CH == iota((heads, width), 0)).astype(BF16)
    hi, lo = split_two(v)
    return bdot(hi, e) + bdot(lo, e)


def lower(n):
    return iota((n, n), 0) >= iota((n, n), 1)


def states_body(x_ref, bc_ref, step_ref, code_ref, rate, st_ref, end_ref, total_ref, cum_ref):
    rows, heads = step_ref.shape
    tri = lower(GROUP).astype(F32)
    total = state = None
    for b in range(rows // GROUP):
        r = pl.ds(b * GROUP, GROUP)
        decay = -jnp.minimum(code_ref[r, :].astype(F32) * rate, 20.0)
        cum = exact_dot(tri, decay)
        cum_ref[r, :] = cum
        last = cum[GROUP - 1 : GROUP, :]
        weight = jnp.exp(last - cum) * step_ref[r, :]
        v = (x_ref[r, :].astype(F32) * spread(weight, heads)).astype(BF16)
        term = lax.dot_general(
            bc_ref[r, : bc_ref.shape[1] // 2], v, (((0,), (0,)), ((), ())), preferred_element_type=F32
        )
        if state is None:
            st_ref[...] = term
            state, total = term, last
        else:
            factor = spread(jnp.broadcast_to(jnp.exp(last), (8, heads)), heads)[0:1]
            state, total = factor * state + term, total + last
    end_ref[...] = state
    wide = jnp.concatenate([total, jnp.zeros((1, 128 - heads), F32)], axis=1)
    total_ref[...] = jnp.broadcast_to(wide, (8, 128))


def diag_pieces(x_ref, bc_ref, step_ref, cum_ref, skip, y_ref):
    rows, heads = step_ref.shape
    n = bc_ref.shape[1] // 2
    half = GROUP // 2
    zero = jnp.zeros((), BF16)

    def piece(b, pairs):
        r = pl.ds(b * GROUP, GROUP)
        eye = (iota((heads, heads), 0) == iota((heads, heads), 1)).astype(F32)
        left = iota((GROUP, 2 * CH), 1) < CH
        gains = spread(jnp.broadcast_to(skip, (8, heads)), heads)[0:1]
        scores = bdot(bc_ref[r, n:], bc_ref[r, :n], NT)
        scores = jnp.where(lower(GROUP), scores, 0.0)
        cum = cum_ref[r, :]
        cum_row = exact_dot(eye, cum, NT)
        step_row = exact_dot(eye, step_ref[r, :], NT)
        for pair in pairs:
            lanes = pl.ds(pair * 2 * CH, 2 * CH)
            xp = x_ref[r, lanes]
            tops, bottoms = [], []
            for side in range(2):
                h = 2 * pair + side
                mine = jnp.where(left if side == 0 else ~left, xp, zero)
                col = cum[:, h : h + 1]
                row = cum_row[h : h + 1, :]
                srow = step_row[h : h + 1, :]
                top = (
                    jnp.exp(jnp.minimum(col[:half] - row[:, :half], 0.0))
                    * scores[:half, :half]
                    * srow[:, :half]
                ).astype(BF16)
                bottom = (
                    jnp.exp(jnp.minimum(col[half:] - row, 0.0)) * scores[half:, :] * srow
                ).astype(BF16)
                tops.append(bdot(top, mine[:half]))
                bottoms.append(bdot(bottom, mine))
            xs = xp.astype(F32) * gains[:, pair * 2 * CH : (pair + 1) * 2 * CH]
            y_ref[pl.ds(b * GROUP, half), lanes] = tops[0] + tops[1] + xs[:half]
            y_ref[pl.ds(b * GROUP + half, half), lanes] = bottoms[0] + bottoms[1] + xs[half:]

    quarter = heads // 4
    return [
        functools.partial(piece, b, range(k * quarter, (k + 1) * quarter))
        for b in range(rows // GROUP)
        for k in range(2)
    ]


def mixed_blocks(bc_ref, cum_ref, prev_ref, st_ref, y_ref):
    rows, heads = cum_ref.shape
    n = bc_ref.shape[1] // 2
    out = []
    high = None
    for b in range(rows // GROUP):
        r = pl.ds(b * GROUP, GROUP)
        c = bc_ref[r, n:]
        cum = cum_ref[r, :]
        if b == 0:
            high = prev_ref[...]
            inner = bdot(c, high)
        else:
            last = cum_ref[pl.ds(GROUP - 8, 8), :]
            factor = spread(jnp.exp(last), heads)[7:8]
            state = factor * high.astype(F32) + st_ref[...]
            hi, lo = split_two(state)
            inner = bdot(c, hi) + bdot(c, lo)
        out.append((r, y_ref[r, :] + inner * spread(jnp.exp(cum), heads)))
    return out


def gate_body(bc_ref, cum_ref, prev_ref, st_ref, y_ref, gate_ref, gain, g_ref, ss_ref):
    ones = jnp.ones((8, g_ref.shape[1]), F32)
    for r, mixed in mixed_blocks(bc_ref, cum_ref, prev_ref, st_ref, y_ref):
        gate = gate_ref[r, :].astype(F32)
        gated = mixed * (gate / (1.0 + jnp.exp(-gate)))
        g_ref[r, :] = (gated * gain).astype(BF16)
        ss_ref[:, r] = exact_dot(ones, gated * gated, NT)


def last_body(bc_ref, cum_ref, prev_ref, st_ref, y_ref, m_ref, ss_ref):
    ones = jnp.ones((8, m_ref.shape[1]), F32)
    for r, mixed in mixed_blocks(bc_ref, cum_ref, prev_ref, st_ref, y_ref):
        m_ref[r, :] = mixed
        ss_ref[:, r] = exact_dot(ones, mixed * mixed, NT)


NC = 8
CHUNK_LAG = 2
MESH = pl.DeviceIdType.MESH
Y, Z, CORES = 4, 8, 2


def place():
    seq = lax.axis_index("seq")
    return seq // (Z * CORES), (seq // CORES) % Z, seq % CORES


def seq_of(y, z, c):
    return (y * Z + z) * CORES + c


class Copies:
    def __init__(self, send_sem, recv_sem):
        self.send_sem, self.recv_sem = send_sem, recv_sem
        self.names = {}
        self.started = []

    def _make(self, name, src, dst, device):
        at = self.names.setdefault(name, len(self.names))
        return pltpu.make_async_remote_copy(
            src_ref=src, dst_ref=dst, send_sem=self.send_sem.at[at], recv_sem=self.recv_sem.at[at],
            device_id=device, device_id_type=MESH,
        )

    def send(self, name, src, dst, device):
        copy = self._make(name, src, dst, device)
        copy.start()
        self.started.append(copy)

    def arrived(self, name, where, device):
        self._make(name, where, where, device).wait_recv()

    def finish(self):
        for copy in self.started:
            copy.wait_send()


def weight_steps(cp, tag, own, w, local_sem):
    y, z, c = place()
    head = lax.axis_index("head")
    half = own.shape[0] // 2
    f = 1 - 2 * c
    top, low = pl.ds(0, half), pl.ds(half, half)

    def at_y(k):
        return lax.rem(y + k * f + 2 * Y, Y)

    def at_z(k):
        return lax.rem(z + k * f + 2 * Z, Z)

    to_y = {k: (seq_of(at_y(k), z, c), head) for k in (1, -1)}
    to_z = {k: (seq_of(y, at_z(k), c), head) for k in (1, -1)}
    other = (seq_of(y, z, 1 - c), head)

    def a_piece(ky):
        return w.at[at_y(ky), z, c, top]

    def a_block(kz):
        return w.at[:, at_z(kz), c, top]

    def b_piece(kz):
        return w.at[y, at_z(kz), c, low]

    def b_block(ky):
        return w.at[at_y(ky), :, c, low]

    def push(name, ref, device):
        cp.send(name, ref, ref, device)

    def a_share(kz):
        push((tag, "as", kz), a_block(kz), other)

    def b_share(ky):
        push((tag, "bs", ky), b_block(ky), other)

    def a_went(way, k):
        cp.arrived((tag, "az", way, k), a_block(-way * (k + 1)), to_z[way])
        if k < (3 if way == 1 else 2):
            push((tag, "az", way, k + 1), a_block(-way * (k + 1)), to_z[way])
        a_share(-way * (k + 1))

    def b_went(way, k):
        cp.arrived((tag, "bz", way, k), b_piece(-way * (k + 1)), to_z[way])
        if k < (3 if way == -1 else 2):
            push((tag, "bz", way, k + 1), b_piece(-way * (k + 1)), to_z[way])

    def s0():
        mine = pltpu.make_async_copy(own, w.at[y, z, c], local_sem)
        mine.start()
        for way in (1, -1):
            cp.send((tag, "ay", way, 0), own.at[top], a_piece(0), to_y[way])
            cp.send((tag, "bz", way, 0), own.at[low], b_piece(0), to_z[way])
        mine.wait()

    def s1():
        cp.arrived((tag, "ay", 1, 0), a_piece(-1), to_y[1])
        push((tag, "ay", 1, 1), a_piece(-1), to_y[1])
        b_went(1, 0)
        b_went(-1, 0)

    def s2():
        cp.arrived((tag, "ay", -1, 0), a_piece(1), to_y[-1])
        cp.arrived((tag, "ay", 1, 1), a_piece(-2), to_y[1])
        for way in (1, -1):
            push((tag, "az", way, 0), a_block(0), to_z[way])
        a_share(0)
        b_went(1, 1)
        b_went(-1, 1)

    def s3():
        b_went(1, 2)
        b_went(-1, 2)
        a_went(1, 0)
        a_went(-1, 0)

    def s4():
        b_went(-1, 3)
        for way in (1, -1):
            push((tag, "by", way, 0), b_block(0), to_y[way])
        b_share(0)
        a_went(1, 1)
        a_went(-1, 1)

    def s5():
        a_went(1, 2)
        a_went(-1, 2)
        cp.arrived((tag, "by", -1, 0), b_block(1), to_y[-1])
        push((tag, "by", -1, 1), b_block(1), to_y[-1])
        b_share(1)
        cp.arrived((tag, "by", 1, 0), b_block(-1), to_y[1])
        b_share(-1)

    def s6():
        a_went(1, 3)
        cp.arrived((tag, "by", -1, 1), b_block(2), to_y[-1])
        b_share(2)

    def s7():
        for kz in range(-4, 4):
            where = w.at[:, lax.rem(z - kz * f + 2 * Z, Z), 1 - c, top]
            cp.arrived((tag, "as", kz), where, other)
        for ky in range(-1, 3):
            where = w.at[lax.rem(y - ky * f + 2 * Y, Y), :, 1 - c, low]
            cp.arrived((tag, "bs", ky), where, other)

    return [s0, s1, s2, s3, s4, s5, s6, s7], [*to_y.values(), *to_z.values(), other]


def prefix_steps(cp, tag, heads, end_ref, total_ref, prev_ref, p):
    y, z, c = place()
    head = lax.axis_index("head")
    other = (seq_of(y, z, 1 - c), head)
    n, width = end_ref.shape
    half, lanes, part = n // 2, width // 2, heads // 2
    to_z = {k: (seq_of(y, lax.rem(z + k, Z), c), head) for k in range(1, Z)}
    to_y = {k: (seq_of(lax.rem(y + k, Y), z, c), head) for k in range(1, Y)}
    mine = pl.ds(pl.multiple_of(c * half, half), half)
    theirs = pl.ds(pl.multiple_of((1 - c) * half, half), half)
    first = c == 0

    def cell(j):
        return pl.ds((j // 2) * 16, 16), pl.ds((j % 2) * lanes, lanes)

    def factor(log):
        return spread(jnp.exp(log), part)

    def log_of(tail):
        return tail[:, :part] + tail[:, part : 2 * part] + tail[:, 2 * part : 3 * part]

    def core_out():
        p.pair_out[pl.ds(0, half), :] = end_ref[theirs, :]
        p.pair_out[pl.ds(half, 8), pl.ds(0, 128)] = total_ref[...]
        p.pair_out[pl.ds(half, 8), pl.ds(128, width - 128)] = jnp.zeros((8, width - 128), F32)
        cp.send((tag, "out"), p.pair_out, p.pair_in, other)

    def z_out():
        cp.arrived((tag, "out"), p.pair_in, other)
        own, got = end_ref[mine, :], p.pair_in[pl.ds(0, half), :]
        own_log = total_ref[:, :heads]
        got_log = p.pair_in[pl.ds(half, 8), pl.ds(0, 128)][:, :heads]
        s0, s1 = jnp.where(first, own, got), jnp.where(first, got, own)
        log0, log1 = jnp.where(first, own_log, got_log), jnp.where(first, got_log, own_log)
        p.zero_state[...] = s0
        p.zero_factor[...] = spread(jnp.exp(log0), heads)
        chip = spread(jnp.exp(log1), heads)[0:1] * s0 + s1
        log = log0 + log1
        log = jnp.concatenate([log, log], axis=0)
        for j in range(Z):
            r, q = cell(j)
            p.z_out[j, :, pl.ds(0, lanes)] = chip[r.start : r.start + 16, q.start : q.start + lanes].astype(BF16)
            rest = log[:, (j % 2) * part : (j % 2 + 1) * part]
            pieces = []
            for _ in range(3):
                piece = rest.astype(BF16).astype(F32)
                pieces.append(piece)
                rest = rest - piece
            pieces.append(jnp.zeros((16, 128 - 3 * part), F32))
            p.z_out[j, :, pl.ds(lanes, 128)] = jnp.concatenate(pieces, axis=1).astype(BF16)
        for k in range(1, Z):
            cp.send((tag, "z", k), p.z_out.at[lax.rem(z + k, Z)], p.z_in.at[z], to_z[k])
        p.z_in[z] = p.z_out[z]

    def y_out():
        for k in range(1, Z):
            cp.arrived((tag, "z", k), p.z_in.at[lax.rem(z - k + Z, Z)], to_z[k])
        run = jnp.zeros((16, lanes), F32)
        logs = jnp.zeros((16, part), F32)
        for j in range(Z):
            log = log_of(p.z_in[j, :, pl.ds(lanes, 128)].astype(F32))
            f = factor(log)
            p.z_factor[j] = f
            run = f * run + p.z_in[j, :, pl.ds(0, lanes)].astype(F32)
            logs = logs + log
        p.y_in[y, :, pl.ds(0, lanes)] = run
        p.y_in[y, :, pl.ds(lanes, 128)] = jnp.concatenate([logs, jnp.zeros((16, 128 - part), F32)], axis=1)
        for k in range(1, Y):
            cp.send((tag, "y", k), p.y_in.at[y], p.y_in.at[y], to_y[k])

    def z_back():
        for k in range(1, Y):
            cp.arrived((tag, "y", k), p.y_in.at[lax.rem(y - k + Y, Y)], to_y[k])
        run = jnp.zeros((16, lanes), F32)
        for j in range(Y):
            f = factor(p.y_in[j, :, pl.ds(lanes, 128)][:, :part])
            run = jnp.where(j < y, f * run + p.y_in[j, :, pl.ds(0, lanes)], run)
        for j in range(Z):
            p.back_out[j] = run.astype(BF16)
            run = p.z_factor[j] * run + p.z_in[j, :, pl.ds(0, lanes)].astype(F32)
        for k in range(1, Z):
            cp.send((tag, "b", k), p.back_out.at[lax.rem(z + k, Z)], p.back_in.at[z], to_z[k])
        p.back_in[z] = p.back_out[z]

    def core_back():
        for k in range(1, Z):
            cp.arrived((tag, "b", k), p.back_in.at[lax.rem(z - k + Z, Z)], to_z[k])
        rows = [
            jnp.concatenate([p.back_in[2 * i], p.back_in[2 * i + 1]], axis=1) for i in range(Z // 2)
        ]
        zero = jnp.concatenate(rows, axis=0).astype(F32)
        one = p.zero_factor[0:1, :] * zero + p.zero_state[...]
        p.core_out[...] = jnp.where(first, one, zero).astype(BF16)
        cp.send((tag, "core"), p.core_out, prev_ref.at[mine], other)
        prev_ref[mine, :] = jnp.where(first, zero, one).astype(BF16)

    def done():
        cp.arrived((tag, "core"), prev_ref.at[theirs], other)

    return [core_out, z_out, y_out, z_back, core_back, done], [*to_z.values(), *to_y.values(), other]


N_PREFIX_COPIES = 2 * Z + Y - 1


N_WEIGHT_COPIES = 32


def greet(devices):
    barrier = pltpu.get_barrier_semaphore()
    for device in devices:
        pl.semaphore_signal(barrier, inc=1, device_id=device, device_id_type=MESH)
    pl.semaphore_wait(barrier, len(devices))


def mixer_body(names, *refs):
    a = types.SimpleNamespace(**dict(zip(names, refs)))
    rows, width = a.x_in.shape
    heads = a.step_in.shape[1]
    states = a.bc_in.shape[1]
    seq, me = lax.axis_index("seq"), lax.axis_index("head")
    n_seq, n_head = lax.axis_size("seq"), lax.axis_size("head")
    depth = width * n_head
    r, o, l = (lax.rem(me + k, n_head) for k in (1, 2, 3))
    right, opposite, left = ((seq, k) for k in (r, o, l))
    after, before = ((lax.rem(seq + k, n_seq), me) for k in (1, n_seq - 1))
    across = ((1, right), (2, opposite), (3, left))
    cp = Copies(a.send_sem, a.recv_sem)
    out_steps, _ = weight_steps(cp, "wo", a.w_out, a.wo, a.local_sem.at[0])
    steps, _ = weight_steps(cp, "wi", a.w_in, a.wi, a.local_sem.at[1])

    def prefix_of(layer):
        views = {k: getattr(a, k).at[layer] for k in PREFIX_NAMES}
        return prefix_steps(
            cp, ("prefix", layer), heads, a.end, a.total, a.prev.at[layer], types.SimpleNamespace(**views)
        )

    prefix, partners = prefix_of(0)
    greet([right, opposite, left, after, before, *partners])

    def turn(work):
        if work:
            work.pop(0)()

    turn(out_steps)
    states_body(a.x_in, a.bc_in, a.step_in, a.code.at[0], a.rate[0:1, :], a.st, a.end, a.total, a.cum)
    turn(prefix)
    turn(out_steps)
    diag = diag_pieces(a.x_in, a.bc_in, a.step_in, a.cum, a.skip[0:1, :], a.own)
    while prefix:
        turn(diag)
        turn(prefix)
        turn(out_steps)
    gate_body(a.bc_in, a.cum, a.prev.at[0], a.st, a.own, a.gate, a.norm_gain[...], a.g, a.ss.at[0])
    for k, device in across:
        cp.send(("ss", k), a.ss.at[0], a.ss_in.at[k - 1], device)
    while out_steps:
        turn(out_steps)
    turn(steps)

    g_ref, wo_ref, resid_ref, gain_ref, bias_ref = a.g, a.wo, a.resid_in, a.resid_gain, a.bias
    cx_ref, cbc_ref, out_ref, x_ref, bc_ref, step_ref = a.conv_x, a.conv_bc, a.resid_out, a.x_two, a.bc_two, a.step_two
    w_ref, hid_ref, h_ref, opp_ref, right_ref, left_ref, own_ref = a.wi, a.hid, a.h, a.opp, a.right, a.left, a.own
    sum_r_ref, sum_l_ref, in_l1, in_r1, in_l2, in_r2 = a.sum_r, a.sum_l, a.in_l1, a.in_r1, a.in_l2, a.in_r2
    ss_ref, ss_in, tail_ref, halo_ref, scale_ref, rs_ref, pre_ref = (
        a.ss.at[0], a.ss_in, a.tail, a.halo, a.scale, a.rs, a.pre
    )
    chunk = rows // NC
    half = width // 2
    lo, hi = pl.ds(0, half), pl.ds(half, half)
    order = [NC - 1 - k for k in range(NC)]
    tile = 256

    def cut(c):
        return pl.ds(c * chunk, chunk)

    def product(first, n, dest, store):
        @pl.loop(0, width // tile)
        def _(j):
            at = pl.multiple_of(j * tile, tile)
            weight = wo_ref[dest, pl.ds(j * (Z // 4), Z // 4)].reshape(tile, width)
            store(pl.ds(at, tile), bdot(g_ref[pl.ds(first, n), :], weight, NT))

    def project(k):
        if k % 2:
            return
        first, n = order[k + 1] * chunk, 2 * chunk
        at = pl.ds(first, n)

        def to_opp(cols, p):
            opp_ref[at, cols] = p.astype(BF16)

        def keep(ref):
            def store(cols, p):
                ref[at, cols] = p

            return store

        product(first, n, o, to_opp)
        for c in (order[k], order[k + 1]):
            cp.send(("1r", c), opp_ref.at[cut(c), lo], in_l1.at[cut(c)], right)
            cp.send(("1l", c), opp_ref.at[cut(c), hi], in_r1.at[cut(c)], left)
        product(first, n, r, keep(right_ref))
        product(first, n, l, keep(left_ref))
        product(first, n, me, keep(own_ref))

    def second_sum(c):
        q = cut(c)
        cp.arrived(("1r", c), in_l1.at[q], right)
        sum_r_ref[q, lo] = (right_ref[q, lo] + in_l1[q, :].astype(F32)).astype(BF16)
        sum_r_ref[q, hi] = right_ref[q, hi].astype(BF16)
        cp.send(("2r", c), sum_r_ref.at[q], in_l2.at[q], right)
        cp.arrived(("1l", c), in_r1.at[q], left)
        sum_l_ref[q, hi] = (left_ref[q, hi] + in_r1[q, :].astype(F32)).astype(BF16)
        sum_l_ref[q, lo] = left_ref[q, lo].astype(BF16)
        cp.send(("2l", c), sum_l_ref.at[q], in_r2.at[q], left)

    def token_scale(tag, ss_ref, ss_in):
        for k, device in across:
            cp.arrived((tag, k), ss_in.at[k - 1], device)
        total = ss_ref[...] + ss_in[0] + ss_in[1] + ss_in[2]
        eighth = jnp.full((8, 128), 0.125, F32)
        column = exact_dot(total, eighth, (((0,), (0,)), ((), ())))
        scale_ref[...] = lax.rsqrt(column / depth + 1e-05)

    def residual(c):
        q = cut(c)
        cp.arrived(("2r", c), in_l2.at[q], right)
        cp.arrived(("2l", c), in_r2.at[q], left)
        total = own_ref[q, :] + in_l2[q, :].astype(F32) + in_r2[q, :].astype(F32)
        total = total * scale_ref[q, 0:1] + resid_ref[q, :].astype(F32)
        out_ref[q, :] = total.astype(BF16)
        hid_ref[me, q, :] = out_ref[q, :]
        cp.send(("3r", c), hid_ref.at[me, q], hid_ref.at[me, q], right)
        cp.send(("3l", c), hid_ref.at[me, q], hid_ref.at[me, q], left)

    def hand_on(c):
        q = cut(c)
        cp.arrived(("3r", c), hid_ref.at[l, q], right)
        cp.send(("4r", c), hid_ref.at[l, q, lo], hid_ref.at[l, q, lo], right)
        cp.arrived(("3l", c), hid_ref.at[r, q], left)
        cp.send(("4l", c), hid_ref.at[r, q, hi], hid_ref.at[r, q, hi], left)

    def scaled(src, q, at, n, keep):
        parts = [src[k, q, :].astype(F32) for k in range(n_head)]
        total = sum(jnp.sum(v * v, axis=1, keepdims=True) for v in parts)
        rs = lax.rsqrt(total / depth + 1e-05)
        rs_ref[pl.ds(at, n), :] = jnp.broadcast_to(rs if keep is None else rs * keep, (n, 128))
        for k, v in enumerate(parts):
            h_ref[k, pl.ds(at, n), :] = (v * gain_ref[:, k * width : (k + 1) * width]).astype(BF16)

    def complete(c):
        q = cut(c)
        cp.arrived(("4r", c), hid_ref.at[o, q, lo], right)
        cp.arrived(("4l", c), hid_ref.at[o, q, hi], left)
        if c == NC - 1:
            tail_ref[...] = hid_ref[:, pl.ds(rows - HALO, HALO), :]
            cp.send("halo", tail_ref, halo_ref, after)
        scaled(hid_ref, q, c * chunk + HALO, chunk, None)

    for t in range(NC + 4 * CHUNK_LAG):
        for stage, work in reversed(list(enumerate((project, second_sum, residual, hand_on, complete)))):
            k = t - CHUNK_LAG * stage
            if 0 <= k < NC:
                if work is residual and k == 0:
                    token_scale("ss", ss_ref, ss_in)
                work(k if work is project else order[k])
        if steps:
            steps.pop(0)()
    while steps:
        steps.pop(0)()
    cp.arrived("halo", halo_ref, after)
    scaled(halo_ref, pl.ds(0, HALO), 0, HALO, jnp.where(seq == 0, 0.0, 1.0))

    def into(cols, at, n):
        total = None
        for k in range(n_head):
            piece = bdot(
                h_ref[k, pl.ds(at, n), :], w_ref[k, :, :, :, cols].reshape(width, cols.size)
            )
            total = piece if total is None else total + piece
        return total

    def conv(taps, k):
        n = taps.shape[1]
        total = None
        for tap in range(k):
            v = pre_ref[pl.ds(HALO - k + 1 + tap, rows), :n] * taps[tap : tap + 1, :].astype(F32)
            total = v if total is None else total + v
        return (total / (1.0 + jnp.exp(-total))).astype(BF16)

    every = rows + HALO

    def pre(cols):
        rs = rs_ref[...]
        pre_ref[...] = (into(cols, 0, every) * jnp.concatenate([rs, rs], axis=1)).astype(BF16).astype(F32)

    @pl.loop(0, width // tile)
    def _(i):
        cols = pl.ds(pl.multiple_of(i * tile, tile), tile)
        pre(cols)
        x_ref[:, cols] = conv(cx_ref[:, cols], cx_ref.shape[0])

    pre(pl.ds(width, states))
    bc_ref[...] = conv(cbc_ref[...], cbc_ref.shape[0])
    dt = into(pl.ds(width + states, 128), HALO, rows)
    dt = (dt * rs_ref[pl.ds(HALO, rows), :])[:, :heads] + bias_ref[...]
    step_ref[...] = jnp.maximum(dt, 0.0) + jnp.log(1.0 + jnp.exp(-jnp.abs(dt)))

    states_body(x_ref, bc_ref, step_ref, a.code.at[1], a.rate[1:2, :], a.st, a.end, a.total, a.cum)
    prefix, _ = prefix_of(1)
    turn(prefix)
    diag = diag_pieces(x_ref, bc_ref, step_ref, a.cum, a.skip[1:2, :], a.own)
    while prefix:
        turn(diag)
        turn(prefix)
    last_body(bc_ref, a.cum, a.prev.at[1], a.st, a.own, a.right, a.ss.at[1])
    for k, device in across:
        cp.send(("ss two", k), a.ss.at[1], a.ss_two.at[k - 1], device)
    token_scale("ss two", a.ss.at[1], a.ss_two)
    for c in range(NC):
        q = cut(c)
        a.mixer_out[q, :] = (a.right[q, :] * scale_ref[q, 0:1]).astype(BF16)
    cp.finish()


PREFIX_NAMES = (
    "pair_out", "pair_in", "zero_state", "zero_factor", "z_out", "z_in", "z_factor", "y_in", "back_out", "back_in", "core_out",
)


def mixer(ins, rows, width, heads, states):
    n_head = lax.axis_size("head")
    n = states // 2
    lanes = width // 2
    copies = 2 * N_WEIGHT_COPIES + 2 * N_PREFIX_COPIES + 6 + 1 + 8 * NC
    outs = {"resid_out": sds(rows, width, dtype=BF16), "mixer_out": sds(rows, width, dtype=BF16)}

    def keep(*shape, dtype=F32):
        return pltpu.VMEM(shape, dtype)

    small = functools.partial(keep, dtype=BF16)
    scratch = {
        "wo": small(Y, Z, CORES, *ins["w_out"].shape),
        "wi": small(Y, Z, CORES, *ins["w_in"].shape),
        "hid": small(n_head, rows, width),
        "h": small(n_head, rows + HALO, width),
        "opp": small(rows, width),
        "right": keep(rows, width),
        "left": keep(rows, width),
        "own": keep(rows, width),
        "sum_r": small(rows, width),
        "sum_l": small(rows, width),
        "in_l1": small(rows, lanes),
        "in_r1": small(rows, lanes),
        "in_l2": small(rows, width),
        "in_r2": small(rows, width),
        "g": small(rows, width),
        "x_two": small(rows, width),
        "bc_two": small(rows, states),
        "step_two": keep(rows, heads),
        "cum": keep(rows, heads),
        "st": keep(n, width),
        "end": keep(n, width),
        "total": keep(8, 128),
        "prev": small(2, n, width),
        "ss": keep(2, 8, rows),
        "ss_in": keep(3, 8, rows),
        "ss_two": keep(3, 8, rows),
        "tail": small(n_head, HALO, width),
        "halo": small(n_head, HALO, width),
        "scale": keep(rows, 128),
        "rs": keep(rows + HALO, 128),
        "pre": keep(rows + HALO, 256),
        "pair_out": keep(2, n // 2 + 8, width),
        "pair_in": keep(2, n // 2 + 8, width),
        "zero_state": keep(2, n // 2, width),
        "zero_factor": keep(2, 8, width),
        "z_out": small(2, Z, 16, lanes + 128),
        "z_in": small(2, Z, 16, lanes + 128),
        "z_factor": keep(2, Z, 16, lanes),
        "y_in": keep(2, Y, 16, lanes + 128),
        "back_out": small(2, Z, 16, lanes),
        "back_in": small(2, Z, 16, lanes),
        "core_out": small(2, n // 2, width),
        "send_sem": pltpu.SemaphoreType.DMA((copies,)),
        "recv_sem": pltpu.SemaphoreType.DMA((copies,)),
        "local_sem": pltpu.SemaphoreType.DMA((2,)),
    }
    return call(
        functools.partial(mixer_body, (*ins, *outs, *scratch)),
        tuple(outs.values()),
        tuple(ins.values()),
        scratch.values(),
        limit=62,
        collective_id=1,
        has_side_effects=True,
    )


def call(body, outs, args, scratch=(), limit=56, **kw):
    return pl.pallas_call(
        body,
        out_shape=outs,
        in_specs=[VMEM] * len(args),
        out_specs=jax.tree.map(lambda _: VMEM, outs),
        scratch_shapes=list(scratch),
        compiler_params=pltpu.CompilerParams(vmem_limit_bytes=limit * 2**20, **kw),
    )(*args)


def sds(*shape, dtype=F32):
    return jax.ShapeDtypeStruct(shape, dtype)


def on_device(
    x_in, gate_in, bc_in, step_in, decay_code, decay_rate, skip_gain, norm_gain, w_out, resid_in,
    resid_gain, w_in_x, w_in_bc, w_in_dt, step_time_bias, conv_x, conv_bc,
):
    rows, width = x_in.shape
    heads = step_in.shape[1]
    w_in = jnp.concatenate(
        [w_in_x, w_in_bc, jnp.pad(w_in_dt, ((0, 0), (0, 128 - heads)))], axis=1
    )
    ins = {
        "x_in": x_in, "gate": gate_in, "bc_in": bc_in, "step_in": step_in, "code": decay_code, "rate": decay_rate,
        "skip": skip_gain, "norm_gain": norm_gain[None, :], "w_out": w_out.T, "resid_in": resid_in,
        "resid_gain": resid_gain[None, :], "w_in": w_in, "bias": step_time_bias[None, :], "conv_x": conv_x,
        "conv_bc": conv_bc,
    }
    return mixer(ins, rows, width, heads, bc_in.shape[1])


def solution(mesh):
    in_specs = (
        P("seq", "head"), P("seq", "head"), P("seq", None), P("seq", "head"), P(None, "seq", "head"),
        P(None, "head"), P(None, "head"), P("head"), P("head", "seq"), P("seq", "head"), P(),
        P("seq", "head"), P("seq", None), P("seq", "head"), P("head"), P(None, "head"), P(),
    )
    out_specs = (P("seq", "head"), P("seq", "head"))
    return jax.shard_map(
        on_device, mesh=mesh, in_specs=in_specs, out_specs=out_specs, check_vma=False
    )
```

```python
import functools
import types

import jax
import jax.numpy as jnp
from jax import lax
from jax.experimental import pallas as pl
from jax.experimental.pallas import tpu as pltpu
from jax.sharding import PartitionSpec as P

CH = 64
GROUP = 256
F32 = jnp.float32
BF16 = jnp.bfloat16
NT = (((1,), (1,)), ((), ()))
VMEM = pl.BlockSpec(memory_space=pltpu.VMEM)
HALO = 16


def iota(shape, dim):
    return lax.broadcasted_iota(jnp.int32, shape, dim)


def exact_dot(a, b, dims=None):
    if dims is None:
        return jnp.dot(a, b, precision=lax.Precision.HIGHEST, preferred_element_type=F32)
    return lax.dot_general(a, b, dims, precision=lax.Precision.HIGHEST, preferred_element_type=F32)


def bdot(a, b, dims=None):
    if dims is None:
        return jnp.dot(a, b, preferred_element_type=F32)
    return lax.dot_general(a, b, dims, preferred_element_type=F32)


def split_two(v):
    hi = v.astype(BF16)
    return hi, (v - hi.astype(F32)).astype(BF16)


def spread(v, heads):
    width = heads * CH
    e = (iota((heads, width), 1) // CH == iota((heads, width), 0)).astype(BF16)
    hi, lo = split_two(v)
    return bdot(hi, e) + bdot(lo, e)


def lower(n):
    return iota((n, n), 0) >= iota((n, n), 1)


def states_block(b, x_ref, bc_ref, step_ref, code, rate, st_ref, end_ref, total_ref, cum_ref):
    heads = step_ref.shape[1]
    r = pl.ds(b * GROUP, GROUP)
    decay = -jnp.minimum(code.astype(F32).T * rate, 20.0)
    cum = exact_dot(lower(GROUP).astype(F32), decay)
    cum_ref[r, :] = cum
    last = cum[GROUP - 1 : GROUP, :]
    weight = jnp.exp(last - cum) * step_ref[r, :]
    v = (x_ref[r, :].astype(F32) * spread(weight, heads)).astype(BF16)
    term = lax.dot_general(
        bc_ref[r, : bc_ref.shape[1] // 2], v, (((0,), (0,)), ((), ())), preferred_element_type=F32
    )
    if b == 0:
        st_ref[...] = term
        return
    factor = spread(jnp.broadcast_to(jnp.exp(last), (8, heads)), heads)[0:1]
    end_ref[...] = factor * st_ref[...] + term
    total = cum_ref[pl.ds(GROUP - 1, 1), :] + last
    wide = jnp.concatenate([total, jnp.zeros((1, 128 - heads), F32)], axis=1)
    total_ref[...] = jnp.broadcast_to(wide, (8, 128))


def diag_pieces(x_ref, bc_ref, step_ref, cum_ref, skip, y_ref):
    rows, heads = step_ref.shape
    n = bc_ref.shape[1] // 2
    half = GROUP // 2
    zero = jnp.zeros((), BF16)

    def piece(b, pairs):
        r = pl.ds(b * GROUP, GROUP)
        eye = (iota((heads, heads), 0) == iota((heads, heads), 1)).astype(F32)
        left = iota((GROUP, 2 * CH), 1) < CH
        gains = spread(jnp.broadcast_to(skip, (8, heads)), heads)[0:1]
        scores = bdot(bc_ref[r, n:], bc_ref[r, :n], NT)
        scores = jnp.where(lower(GROUP), scores, 0.0)
        cum = cum_ref[r, :]
        cum_row = exact_dot(eye, cum, NT)
        step_row = exact_dot(eye, step_ref[r, :], NT)
        for pair in pairs:
            lanes = pl.ds(pair * 2 * CH, 2 * CH)
            xp = x_ref[r, lanes]
            tops, bottoms = [], []
            for side in range(2):
                h = 2 * pair + side
                mine = jnp.where(left if side == 0 else ~left, xp, zero)
                col = cum[:, h : h + 1]
                row = cum_row[h : h + 1, :]
                srow = step_row[h : h + 1, :]
                top = (
                    jnp.exp(jnp.minimum(col[:half] - row[:, :half], 0.0))
                    * scores[:half, :half]
                    * srow[:, :half]
                ).astype(BF16)
                bottom = (
                    jnp.exp(jnp.minimum(col[half:] - row, 0.0)) * scores[half:, :] * srow
                ).astype(BF16)
                tops.append(bdot(top, mine[:half]))
                bottoms.append(bdot(bottom, mine))
            xs = xp.astype(F32) * gains[:, pair * 2 * CH : (pair + 1) * 2 * CH]
            y_ref[pl.ds(b * GROUP, half), lanes] = tops[0] + tops[1] + xs[:half]
            y_ref[pl.ds(b * GROUP + half, half), lanes] = bottoms[0] + bottoms[1] + xs[half:]

    quarter = heads // 4
    return [
        functools.partial(piece, b, range(k * quarter, (k + 1) * quarter))
        for b in range(rows // GROUP)
        for k in range(2)
    ]


def mixed_blocks(bc_ref, cum_ref, prev_ref, st_ref, y_ref):
    rows, heads = cum_ref.shape
    n = bc_ref.shape[1] // 2
    out = []
    high = None
    for b in range(rows // GROUP):
        r = pl.ds(b * GROUP, GROUP)
        c = bc_ref[r, n:]
        cum = cum_ref[r, :]
        if b == 0:
            high = prev_ref[...]
            inner = bdot(c, high)
        else:
            last = cum_ref[pl.ds(GROUP - 8, 8), :]
            factor = spread(jnp.exp(last), heads)[7:8]
            state = factor * high.astype(F32) + st_ref[...]
            hi, lo = split_two(state)
            inner = bdot(c, hi) + bdot(c, lo)
        out.append((r, y_ref[r, :] + inner * spread(jnp.exp(cum), heads)))
    return out


def squares(v):
    sq = v * v
    part = sum(sq[:, k : k + 128] for k in range(128, v.shape[1], 128)) + sq[:, :128]
    return exact_dot(jnp.ones((8, 128), F32), part, NT)


def gate_body(bc_ref, cum_ref, prev_ref, st_ref, y_ref, gate_ref, gain, g_ref, ss_ref):
    for r, mixed in mixed_blocks(bc_ref, cum_ref, prev_ref, st_ref, y_ref):
        gate = gate_ref[r, :].astype(F32)
        gated = mixed * (gate / (1.0 + jnp.exp(-gate)))
        g_ref[r, :] = (gated * gain).astype(BF16)
        ss_ref[:, r] = squares(gated)


def last_body(bc_ref, cum_ref, prev_ref, st_ref, y_ref, m_ref, ss_ref):
    for r, mixed in mixed_blocks(bc_ref, cum_ref, prev_ref, st_ref, y_ref):
        m_ref[r, :] = mixed
        ss_ref[:, r] = squares(mixed)


NC = 8
CHUNK_LAG = 2
MESH = pl.DeviceIdType.MESH
Y, Z, CORES = 4, 8, 2


def place():
    seq = lax.axis_index("seq")
    return seq // (Z * CORES), (seq // CORES) % Z, seq % CORES


def seq_of(y, z, c):
    return (y * Z + z) * CORES + c


class Copies:
    def __init__(self, send_sem, recv_sem):
        self.send_sem, self.recv_sem = send_sem, recv_sem
        self.names = {}
        self.started = []

    def _make(self, name, src, dst, device):
        at = self.names.setdefault(name, len(self.names))
        return pltpu.make_async_remote_copy(
            src_ref=src, dst_ref=dst, send_sem=self.send_sem.at[at], recv_sem=self.recv_sem.at[at],
            device_id=device, device_id_type=MESH,
        )

    def send(self, name, src, dst, device):
        copy = self._make(name, src, dst, device)
        copy.start()
        self.started.append(copy)

    def arrived(self, name, where, device):
        self._make(name, where, where, device).wait_recv()

    def finish(self):
        for copy in self.started:
            copy.wait_send()


def weight_steps(cp, tag, own, w, local_sem, a_rows):
    y, z, c = place()
    head = lax.axis_index("head")
    f = 1 - 2 * c
    top, low = pl.ds(0, a_rows), pl.ds(a_rows, own.shape[0] - a_rows)

    def at_y(k):
        return lax.rem(y + k * f + 2 * Y, Y)

    def at_z(k):
        return lax.rem(z + k * f + 2 * Z, Z)

    to_y = {k: (seq_of(at_y(k), z, c), head) for k in (1, -1)}
    to_z = {k: (seq_of(y, at_z(k), c), head) for k in (1, -1)}
    other = (seq_of(y, z, 1 - c), head)

    def a_piece(ky):
        return w.at[at_y(ky), z, c, top]

    def a_block(kz):
        return w.at[:, at_z(kz), c, top]

    def b_piece(ky, kz):
        return w.at[at_y(ky), at_z(kz), c, low]

    def b_block(ky):
        return w.at[at_y(ky), :, c, low]

    def push(name, ref, device):
        cp.send((tag, *name), ref, ref, device)

    def here(name, ref, device):
        cp.arrived((tag, *name), ref, device)

    def a_share(kz):
        push(("as", kz), a_block(kz), other)

    def b_share(ky):
        push(("bs", ky), b_block(ky), other)

    def a_went(way, k):
        kz = -way * (k + 1)
        here(("az", way, k), a_block(kz), to_z[way])
        if k < (3 if way == 1 else 2):
            push(("az", way, k + 1), a_block(kz), to_z[way])
        a_share(kz)

    def b_went(way, k):
        kz = -way * (k + 1)
        here(("bz", way, k), b_piece(0, kz), to_z[way])
        if k < (3 if way == -1 else 2):
            push(("bz", way, k + 1), b_piece(0, kz), to_z[way])
        for along in (-1, 1):
            push(("by", along, kz), b_piece(0, kz), to_y[along])

    def b_on(kz):
        here(("by", -1, kz), b_piece(1, kz), to_y[-1])
        push(("bf", kz), b_piece(1, kz), to_y[-1])

    def s0():
        mine = pltpu.make_async_copy(own, w.at[y, z, c], local_sem)
        mine.start()
        for way in (1, -1):
            cp.send((tag, "ay", way, 0), own.at[top], a_piece(0), to_y[way])
            cp.send((tag, "bz", way, 0), own.at[low], b_piece(0, 0), to_z[way])
        for way in (-1, 1):
            cp.send((tag, "by", way, 0), own.at[low], b_piece(0, 0), to_y[way])
        mine.wait()

    def s1():
        here(("ay", 1, 0), a_piece(-1), to_y[1])
        push(("ay", 1, 1), a_piece(-1), to_y[1])
        b_went(1, 0)
        b_went(-1, 0)

    def s2():
        b_on(0)
        b_went(1, 1)
        b_went(-1, 1)
        here(("ay", -1, 0), a_piece(1), to_y[-1])
        here(("ay", 1, 1), a_piece(-2), to_y[1])
        for way in (1, -1):
            push(("az", way, 0), a_block(0), to_z[way])
        a_share(0)

    def s3():
        b_went(1, 2)
        b_went(-1, 2)
        b_on(-1)
        b_on(1)
        a_went(1, 0)
        a_went(-1, 0)

    def s4():
        b_went(-1, 3)
        b_on(-2)
        b_on(2)
        b_share(0)
        a_went(1, 1)
        a_went(-1, 1)

    def s5():
        b_on(-3)
        b_on(3)
        a_went(1, 2)
        a_went(-1, 2)

    def s6():
        b_on(4)
        b_share(1)
        a_went(1, 3)
        for kz in range(-3, 5):
            here(("by", 1, kz), b_piece(-1, kz), to_y[1])
        b_share(-1)

    def s7():
        for kz in range(-3, 5):
            here(("bf", kz), b_piece(2, kz), to_y[-1])
        b_share(2)

    def s8():
        for kz in range(-4, 4):
            here(("as", kz), w.at[:, lax.rem(z - kz * f + 2 * Z, Z), 1 - c, top], other)
        for ky in range(-1, 3):
            here(("bs", ky), w.at[lax.rem(y - ky * f + 2 * Y, Y), :, 1 - c, low], other)

    return [s0, s1, s2, s3, s4, s5, s6, s7, s8]


def prefix_steps(cp, tag, heads, end_ref, total_ref, prev_ref, p):
    y, z, c = place()
    head = lax.axis_index("head")
    other = (seq_of(y, z, 1 - c), head)
    n, width = end_ref.shape
    half, lanes, part = n // 2, width // 2, heads // 2
    to_z = {k: (seq_of(y, lax.rem(z + k, Z), c), head) for k in range(1, Z)}
    to_y = {k: (seq_of(lax.rem(y + k, Y), z, c), head) for k in range(1, Y)}
    mine = pl.ds(pl.multiple_of(c * half, half), half)
    theirs = pl.ds(pl.multiple_of((1 - c) * half, half), half)
    first = c == 0

    def cell(j):
        return pl.ds((j // 2) * 16, 16), pl.ds((j % 2) * lanes, lanes)

    def factor(log):
        return spread(jnp.exp(log), part)

    def log_of(tail):
        return tail[:, :part] + tail[:, part : 2 * part] + tail[:, 2 * part : 3 * part]

    def core_out():
        p.pair_out[pl.ds(0, half), :] = end_ref[theirs, :]
        p.pair_out[pl.ds(half, 8), pl.ds(0, 128)] = total_ref[...]
        p.pair_out[pl.ds(half, 8), pl.ds(128, width - 128)] = jnp.zeros((8, width - 128), F32)
        cp.send((tag, "out"), p.pair_out, p.pair_in, other)

    def z_out():
        cp.arrived((tag, "out"), p.pair_in, other)
        own, got = end_ref[mine, :], p.pair_in[pl.ds(0, half), :]
        own_log = total_ref[:, :heads]
        got_log = p.pair_in[pl.ds(half, 8), pl.ds(0, 128)][:, :heads]
        s0, s1 = jnp.where(first, own, got), jnp.where(first, got, own)
        log0, log1 = jnp.where(first, own_log, got_log), jnp.where(first, got_log, own_log)
        p.zero_state[...] = s0
        p.zero_factor[...] = spread(jnp.exp(log0), heads)
        chip = spread(jnp.exp(log1), heads)[0:1] * s0 + s1
        log = log0 + log1
        log = jnp.concatenate([log, log], axis=0)
        for j in range(Z):
            r, q = cell(j)
            p.z_out[j, :, pl.ds(0, lanes)] = chip[r.start : r.start + 16, q.start : q.start + lanes].astype(BF16)
            rest = log[:, (j % 2) * part : (j % 2 + 1) * part]
            pieces = []
            for _ in range(3):
                piece = rest.astype(BF16).astype(F32)
                pieces.append(piece)
                rest = rest - piece
            pieces.append(jnp.zeros((16, 128 - 3 * part), F32))
            p.z_out[j, :, pl.ds(lanes, 128)] = jnp.concatenate(pieces, axis=1).astype(BF16)
        for k in range(1, Z):
            cp.send((tag, "z", k), p.z_out.at[lax.rem(z + k, Z)], p.z_in.at[z], to_z[k])
        p.z_in[z] = p.z_out[z]

    def y_out():
        for k in range(1, Z):
            cp.arrived((tag, "z", k), p.z_in.at[lax.rem(z - k + Z, Z)], to_z[k])
        run = jnp.zeros((16, lanes), F32)
        logs = jnp.zeros((16, part), F32)
        for j in range(Z):
            log = log_of(p.z_in[j, :, pl.ds(lanes, 128)].astype(F32))
            f = factor(log)
            p.z_factor[j] = f
            run = f * run + p.z_in[j, :, pl.ds(0, lanes)].astype(F32)
            logs = logs + log
        p.y_in[y, :, pl.ds(0, lanes)] = run
        p.y_in[y, :, pl.ds(lanes, 128)] = jnp.concatenate([logs, jnp.zeros((16, 128 - part), F32)], axis=1)
        for k in range(1, Y):
            cp.send((tag, "y", k), p.y_in.at[y], p.y_in.at[y], to_y[k])

    def z_back():
        for k in range(1, Y):
            cp.arrived((tag, "y", k), p.y_in.at[lax.rem(y - k + Y, Y)], to_y[k])
        run = jnp.zeros((16, lanes), F32)
        for j in range(Y):
            f = factor(p.y_in[j, :, pl.ds(lanes, 128)][:, :part])
            run = jnp.where(j < y, f * run + p.y_in[j, :, pl.ds(0, lanes)], run)
        for j in range(Z):
            p.back_out[j] = run.astype(BF16)
            run = p.z_factor[j] * run + p.z_in[j, :, pl.ds(0, lanes)].astype(F32)
        for k in range(1, Z):
            cp.send((tag, "b", k), p.back_out.at[lax.rem(z + k, Z)], p.back_in.at[z], to_z[k])
        p.back_in[z] = p.back_out[z]

    def core_back():
        for k in range(1, Z):
            cp.arrived((tag, "b", k), p.back_in.at[lax.rem(z - k + Z, Z)], to_z[k])
        rows = [
            jnp.concatenate([p.back_in[2 * i], p.back_in[2 * i + 1]], axis=1) for i in range(Z // 2)
        ]
        zero = jnp.concatenate(rows, axis=0).astype(F32)
        one = p.zero_factor[0:1, :] * zero + p.zero_state[...]
        p.core_out[...] = jnp.where(first, one, zero).astype(BF16)
        cp.send((tag, "core"), p.core_out, prev_ref.at[mine], other)
        prev_ref[mine, :] = jnp.where(first, zero, one).astype(BF16)

    def done():
        cp.arrived((tag, "core"), prev_ref.at[theirs], other)

    return [core_out, z_out, y_out, z_back, core_back, done], [*to_z.values(), *to_y.values(), other]


N_PREFIX_COPIES = 2 * Z + Y - 1


N_WEIGHT_COPIES = 53


def greet(devices):
    barrier = pltpu.get_barrier_semaphore()
    for device in devices:
        pl.semaphore_signal(barrier, inc=1, device_id=device, device_id_type=MESH)
    pl.semaphore_wait(barrier, len(devices))


def mixer_body(names, *refs):
    a = types.SimpleNamespace(**dict(zip(names, refs)))
    rows, width = a.x_in.shape
    heads = a.step_in.shape[0]
    states = a.bc_in.shape[1]
    seq, me = lax.axis_index("seq"), lax.axis_index("head")
    n_seq, n_head = lax.axis_size("seq"), lax.axis_size("head")
    depth = width * n_head
    r, o, l = (lax.rem(me + k, n_head) for k in (1, 2, 3))
    right, opposite, left = ((seq, k) for k in (r, o, l))
    after, before = ((lax.rem(seq + k, n_seq), me) for k in (1, n_seq - 1))
    across = ((1, right), (2, opposite), (3, left))
    cp = Copies(a.send_sem, a.recv_sem)
    out_steps = weight_steps(cp, "wo", a.w_out, a.wo, a.local_sem.at[0], 16)
    steps = weight_steps(cp, "wi", a.w_in, a.wi, a.local_sem.at[1], 32)

    def prefix_of(layer):
        views = {k: getattr(a, k).at[layer] for k in PREFIX_NAMES}
        return prefix_steps(
            cp, ("prefix", layer), heads, a.end, a.total, a.prev.at[layer], types.SimpleNamespace(**views)
        )

    prefix, partners = prefix_of(0)
    greet([right, opposite, left, after, before, *partners])

    def turn(work):
        if work:
            work.pop(0)()

    turn(out_steps)
    a.step_one[...] = a.step_in[...].T

    def block_states(layer, b, x_ref, bc_ref, step_ref):
        code = a.code[layer, :, b * GROUP : (b + 1) * GROUP]
        rate = a.rate[layer : layer + 1, :]
        states_block(b, x_ref, bc_ref, step_ref, code, rate, a.st, a.end, a.total, a.cum)

    for b in range(rows // GROUP):
        block_states(0, b, a.x_in, a.bc_in, a.step_one)
    turn(prefix)
    turn(out_steps)
    diag = diag_pieces(a.x_in, a.bc_in, a.step_one, a.cum, a.skip[0:1, :], a.own)
    while prefix:
        turn(diag)
        turn(prefix)
        turn(out_steps)
    gate_body(a.bc_in, a.cum, a.prev.at[0], a.st, a.own, a.gate, a.norm_gain[...], a.g, a.ss.at[0])
    for k, device in across:
        cp.send(("ss", k), a.ss.at[0], a.ss_in.at[k - 1], device)
    while len(out_steps) > 1:
        turn(out_steps)
    turn(steps)
    turn(out_steps)

    g_ref, wo_ref, resid_ref, gain_ref, bias_ref = a.g, a.wo, a.resid_in, a.resid_gain, a.bias
    cx_ref, cbc_ref, out_ref, x_ref, bc_ref, step_ref = a.conv_x, a.conv_bc, a.resid_out, a.x_two, a.bc_two, a.step_two
    w_ref, hid_ref, h_ref, opp_ref, right_ref, left_ref, own_ref = a.wi, a.hid, a.h, a.opp, a.right, a.left, a.own
    sum_r_ref, sum_l_ref, in_l1, in_r1, in_l2, in_r2 = a.sum_r, a.sum_l, a.in_l1, a.in_r1, a.in_l2, a.in_r2
    ss_ref, ss_in, tail_ref, halo_ref, scale_ref, rs_ref, pre_ref = (
        a.ss.at[0], a.ss_in, a.tail, a.halo, a.scale, a.rs, a.pre
    )
    chunk = rows // NC
    half = width // 2
    lo, hi = pl.ds(0, half), pl.ds(half, half)
    order = [NC - 1, *range(NC - 1)]
    tile = 256

    def cut(c):
        return pl.ds(c * chunk, chunk)

    def product(first, n, dest, store):
        @pl.loop(0, width // tile)
        def _(j):
            at = pl.multiple_of(j * tile, tile)
            weight = wo_ref[dest, pl.ds(j * (Z // 4), Z // 4)].reshape(tile, width)
            store(pl.ds(at, tile), bdot(g_ref[pl.ds(first, n), :], weight, NT))

    def project(k):
        chunks = {0: order[0:1], 1: order[1:2], 2: order[2:4], 4: order[4:6], 6: order[6:8]}.get(k)
        if chunks is None:
            return
        first, n = chunks[0] * chunk, len(chunks) * chunk
        at = pl.ds(first, n)

        def to_opp(cols, p):
            opp_ref[at, cols] = p.astype(BF16)

        def keep(ref):
            def store(cols, p):
                ref[at, cols] = p

            return store

        product(first, n, o, to_opp)
        for c in chunks:
            cp.send(("1r", c), opp_ref.at[cut(c), lo], in_l1.at[cut(c)], right)
            cp.send(("1l", c), opp_ref.at[cut(c), hi], in_r1.at[cut(c)], left)
        product(first, n, r, keep(right_ref))
        product(first, n, l, keep(left_ref))
        product(first, n, me, keep(own_ref))

    def second_sum(c):
        q = cut(c)
        cp.arrived(("1r", c), in_l1.at[q], right)
        sum_r_ref[q, lo] = (right_ref[q, lo] + in_l1[q, :].astype(F32)).astype(BF16)
        sum_r_ref[q, hi] = right_ref[q, hi].astype(BF16)
        cp.send(("2r", c), sum_r_ref.at[q], in_l2.at[q], right)
        cp.arrived(("1l", c), in_r1.at[q], left)
        sum_l_ref[q, hi] = (left_ref[q, hi] + in_r1[q, :].astype(F32)).astype(BF16)
        sum_l_ref[q, lo] = left_ref[q, lo].astype(BF16)
        cp.send(("2l", c), sum_l_ref.at[q], in_r2.at[q], left)

    def token_scale(tag, ss_ref, ss_in):
        for k, device in across:
            cp.arrived((tag, k), ss_in.at[k - 1], device)
        total = ss_ref[...] + ss_in[0] + ss_in[1] + ss_in[2]
        eighth = jnp.full((8, 128), 0.125, F32)
        column = exact_dot(total, eighth, (((0,), (0,)), ((), ())))
        scale_ref[...] = lax.rsqrt(column / depth + 1e-05)

    def residual(c):
        q = cut(c)
        cp.arrived(("2r", c), in_l2.at[q], right)
        cp.arrived(("2l", c), in_r2.at[q], left)
        total = own_ref[q, :] + in_l2[q, :].astype(F32) + in_r2[q, :].astype(F32)
        total = total * scale_ref[q, 0:1] + resid_ref[q, :].astype(F32)
        out_ref[q, :] = total.astype(BF16)
        hid_ref[me, q, :] = out_ref[q, :]
        cp.send(("3r", c), hid_ref.at[me, q], hid_ref.at[me, q], right)
        cp.send(("3l", c), hid_ref.at[me, q], hid_ref.at[me, q], left)

    def hand_on(c):
        q = cut(c)
        cp.arrived(("3r", c), hid_ref.at[l, q], right)
        cp.send(("4r", c), hid_ref.at[l, q, lo], hid_ref.at[l, q, lo], right)
        cp.arrived(("3l", c), hid_ref.at[r, q], left)
        cp.send(("4l", c), hid_ref.at[r, q, hi], hid_ref.at[r, q, hi], left)

    def scaled(src, q, at, n, keep):
        parts = [src[k, q, :].astype(F32) for k in range(n_head)]
        total = sum(jnp.sum(v * v, axis=1, keepdims=True) for v in parts)
        rs = lax.rsqrt(total / depth + 1e-05)
        rs_ref[pl.ds(at, n), :] = jnp.broadcast_to(rs if keep is None else rs * keep, (n, 128))
        for k, v in enumerate(parts):
            h_ref[k, pl.ds(at, n), :] = (v * gain_ref[:, k * width : (k + 1) * width]).astype(BF16)

    def complete(c):
        q = cut(c)
        cp.arrived(("4r", c), hid_ref.at[o, q, lo], right)
        cp.arrived(("4l", c), hid_ref.at[o, q, hi], left)
        if c == NC - 1:
            tail_ref[...] = hid_ref[:, pl.ds(rows - HALO, HALO), :]
            cp.send("halo", tail_ref, halo_ref, after)
        scaled(hid_ref, q, c * chunk + HALO, chunk, None)

    def into(cols, at, n):
        total = None
        for k in range(n_head):
            piece = bdot(
                h_ref[k, pl.ds(at, n), :], w_ref[k, :, :, :, cols].reshape(width, cols.size)
            )
            total = piece if total is None else total + piece
        return total

    def conv(taps, k):
        n = taps.shape[1]
        total = None
        for tap in range(k):
            v = pre_ref[pl.ds(HALO - k + 1 + tap, GROUP), :n] * taps[tap : tap + 1, :].astype(F32)
            total = v if total is None else total + v
        return (total / (1.0 + jnp.exp(-total))).astype(BF16)

    def second_inputs(b):
        at, every = b * GROUP, GROUP + HALO
        r = pl.ds(at, GROUP)

        def pre(cols):
            rs = rs_ref[pl.ds(at, every), :]
            both = jnp.concatenate([rs, rs], axis=1)
            pre_ref[...] = (into(cols, at, every) * both).astype(BF16).astype(F32)

        @pl.loop(0, width // tile)
        def _(i):
            cols = pl.ds(pl.multiple_of(i * tile, tile), tile)
            pre(cols)
            x_ref[r, cols] = conv(cx_ref[:, cols], cx_ref.shape[0])

        pre(pl.ds(width, states))
        bc_ref[r, :] = conv(cbc_ref[...], cbc_ref.shape[0])
        dt = into(pl.ds(width + states, 128), at + HALO, GROUP)
        dt = (dt * rs_ref[pl.ds(at + HALO, GROUP), :])[:, :heads] + bias_ref[...]
        step_ref[r, :] = jnp.maximum(dt, 0.0) + jnp.log(1.0 + jnp.exp(-jnp.abs(dt)))

    diag = diag_pieces(x_ref, bc_ref, step_ref, a.cum, a.skip[1:2, :], a.y_two)

    def first_block(t):
        if t == 4 + 4 * CHUNK_LAG:
            cp.arrived("halo", halo_ref, after)
            scaled(halo_ref, pl.ds(0, HALO), 0, HALO, jnp.where(seq == 0, 0.0, 1.0))
            while steps:
                turn(steps)
            second_inputs(0)
        if t == 5 + 4 * CHUNK_LAG:
            block_states(1, 0, x_ref, bc_ref, step_ref)
        if t >= 6 + 4 * CHUNK_LAG:
            turn(diag)

    for t in range(NC + 4 * CHUNK_LAG):
        for stage, work in reversed(list(enumerate((project, second_sum, residual, hand_on, complete)))):
            k = t - CHUNK_LAG * stage
            if 0 <= k < NC:
                if work is residual and k == 0:
                    token_scale("ss", ss_ref, ss_in)
                work(k if work is project else order[k])
        if t == 1 or t >= 3:
            turn(steps)
        first_block(t)
    second_inputs(1)
    block_states(1, 1, x_ref, bc_ref, step_ref)
    prefix, _ = prefix_of(1)
    turn(prefix)
    while prefix:
        turn(diag)
        turn(prefix)
    last_body(bc_ref, a.cum, a.prev.at[1], a.st, a.y_two, a.right, a.ss.at[1])
    for k, device in across:
        cp.send(("ss two", k), a.ss.at[1], a.ss_two.at[k - 1], device)
    token_scale("ss two", a.ss.at[1], a.ss_two)
    for c in range(NC):
        q = cut(c)
        a.mixer_out[q, :] = (a.right[q, :] * scale_ref[q, 0:1]).astype(BF16)
    cp.finish()


PREFIX_NAMES = (
    "pair_out", "pair_in", "zero_state", "zero_factor", "z_out", "z_in", "z_factor", "y_in", "back_out", "back_in", "core_out",
)


def mixer(ins, rows, width, heads, states):
    n_head = lax.axis_size("head")
    n = states // 2
    lanes = width // 2
    copies = 2 * N_WEIGHT_COPIES + 2 * N_PREFIX_COPIES + 6 + 1 + 8 * NC
    outs = {"resid_out": sds(rows, width, dtype=BF16), "mixer_out": sds(rows, width, dtype=BF16)}

    def keep(*shape, dtype=F32):
        return pltpu.VMEM(shape, dtype)

    small = functools.partial(keep, dtype=BF16)
    scratch = {
        "wo": small(Y, Z, CORES, *ins["w_out"].shape),
        "wi": small(Y, Z, CORES, *ins["w_in"].shape),
        "hid": small(n_head, rows, width),
        "h": small(n_head, rows + HALO, width),
        "opp": small(rows, width),
        "right": keep(rows, width),
        "left": keep(rows, width),
        "own": keep(rows, width),
        "sum_r": small(rows, width),
        "sum_l": small(rows, width),
        "in_l1": small(rows, lanes),
        "in_r1": small(rows, lanes),
        "in_l2": small(rows, width),
        "in_r2": small(rows, width),
        "g": small(rows, width),
        "x_two": small(rows, width),
        "bc_two": small(rows, states),
        "step_two": keep(rows, heads),
        "cum": keep(rows, heads),
        "st": keep(n, width),
        "end": keep(n, width),
        "total": keep(8, 128),
        "prev": small(2, n, width),
        "ss": keep(2, 8, rows),
        "ss_in": keep(3, 8, rows),
        "ss_two": keep(3, 8, rows),
        "tail": small(n_head, HALO, width),
        "halo": small(n_head, HALO, width),
        "scale": keep(rows, 128),
        "rs": keep(rows + HALO, 128),
        "pre": keep(GROUP + HALO, 256),
        "y_two": keep(rows, width),
        "step_one": keep(rows, heads),
        "pair_out": keep(2, n // 2 + 8, width),
        "pair_in": keep(2, n // 2 + 8, width),
        "zero_state": keep(2, n // 2, width),
        "zero_factor": keep(2, 8, width),
        "z_out": small(2, Z, 16, lanes + 128),
        "z_in": small(2, Z, 16, lanes + 128),
        "z_factor": keep(2, Z, 16, lanes),
        "y_in": keep(2, Y, 16, lanes + 128),
        "back_out": small(2, Z, 16, lanes),
        "back_in": small(2, Z, 16, lanes),
        "core_out": small(2, n // 2, width),
        "send_sem": pltpu.SemaphoreType.DMA((copies,)),
        "recv_sem": pltpu.SemaphoreType.DMA((copies,)),
        "local_sem": pltpu.SemaphoreType.DMA((2,)),
    }
    return call(
        functools.partial(mixer_body, (*ins, *outs, *scratch)),
        tuple(outs.values()),
        tuple(ins.values()),
        scratch.values(),
        limit=62,
        collective_id=1,
        has_side_effects=True,
    )


def call(body, outs, args, scratch=(), limit=56, **kw):
    return pl.pallas_call(
        body,
        out_shape=outs,
        in_specs=[VMEM] * len(args),
        out_specs=jax.tree.map(lambda _: VMEM, outs),
        scratch_shapes=list(scratch),
        compiler_params=pltpu.CompilerParams(vmem_limit_bytes=limit * 2**20, **kw),
    )(*args)


def sds(*shape, dtype=F32):
    return jax.ShapeDtypeStruct(shape, dtype)


def on_device(
    x_in, gate_in, bc_in, step_in, decay_code, decay_rate, skip_gain, norm_gain, w_out, resid_in,
    resid_gain, w_in_x, w_in_bc, w_in_dt, step_time_bias, conv_x, conv_bc,
):
    rows, width = x_in.shape
    heads = step_in.shape[1]
    w_in = jnp.concatenate(
        [w_in_x, w_in_bc, jnp.pad(w_in_dt, ((0, 0), (0, 128 - heads)))], axis=1
    )
    ins = {
        "x_in": x_in, "gate": gate_in, "bc_in": bc_in, "step_in": step_in.T, "code": jnp.swapaxes(decay_code, 1, 2), "rate": decay_rate,
        "skip": skip_gain, "norm_gain": norm_gain[None, :], "w_out": w_out.T, "resid_in": resid_in,
        "resid_gain": resid_gain[None, :], "w_in": w_in, "bias": step_time_bias[None, :], "conv_x": conv_x,
        "conv_bc": conv_bc,
    }
    return mixer(ins, rows, width, heads, bc_in.shape[1])


def solution(mesh):
    in_specs = (
        P("seq", "head"), P("seq", "head"), P("seq", None), P("seq", "head"), P(None, "seq", "head"),
        P(None, "head"), P(None, "head"), P("head"), P("head", "seq"), P("seq", "head"), P(),
        P("seq", "head"), P("seq", None), P("seq", "head"), P("head"), P(None, "head"), P(),
    )
    out_specs = (P("seq", "head"), P("seq", "head"))
    return jax.shard_map(
        on_device, mesh=mesh, in_specs=in_specs, out_specs=out_specs, check_vma=False
    )
```

```python
import functools
import types

import jax
import jax.numpy as jnp
from jax import lax
from jax.experimental import pallas as pl
from jax.experimental.pallas import tpu as pltpu
from jax.sharding import PartitionSpec as P

CH = 64
GROUP = 256
F32 = jnp.float32
BF16 = jnp.bfloat16
NT = (((1,), (1,)), ((), ()))
VMEM = pl.BlockSpec(memory_space=pltpu.VMEM)
HALO = 16


def iota(shape, dim):
    return lax.broadcasted_iota(jnp.int32, shape, dim)


def exact_dot(a, b, dims=None):
    if dims is None:
        return jnp.dot(a, b, precision=lax.Precision.HIGHEST, preferred_element_type=F32)
    return lax.dot_general(a, b, dims, precision=lax.Precision.HIGHEST, preferred_element_type=F32)


def bdot(a, b, dims=None):
    if dims is None:
        return jnp.dot(a, b, preferred_element_type=F32)
    return lax.dot_general(a, b, dims, preferred_element_type=F32)


def split_two(v):
    hi = v.astype(BF16)
    return hi, (v - hi.astype(F32)).astype(BF16)


def spread(v, heads):
    width = heads * CH
    e = (iota((heads, width), 1) // CH == iota((heads, width), 0)).astype(BF16)
    hi, lo = split_two(v)
    return bdot(hi, e) + bdot(lo, e)


def lower(n):
    return iota((n, n), 0) >= iota((n, n), 1)


def states_block(b, x_ref, bc_ref, step_ref, code, rate, st_ref, end_ref, total_ref, cum_ref):
    heads = step_ref.shape[1]
    r = pl.ds(b * GROUP, GROUP)
    decay = -jnp.minimum(code.astype(F32).T * rate, 20.0)
    cum = exact_dot(lower(GROUP).astype(F32), decay)
    cum_ref[r, :] = cum
    last = cum[GROUP - 1 : GROUP, :]
    weight = jnp.exp(last - cum) * step_ref[r, :]
    v = (x_ref[r, :].astype(F32) * spread(weight, heads)).astype(BF16)
    term = lax.dot_general(
        bc_ref[r, : bc_ref.shape[1] // 2], v, (((0,), (0,)), ((), ())), preferred_element_type=F32
    )
    if b == 0:
        st_ref[...] = term
        return
    factor = spread(jnp.broadcast_to(jnp.exp(last), (8, heads)), heads)[0:1]
    end_ref[...] = factor * st_ref[...] + term
    total = cum_ref[pl.ds(GROUP - 1, 1), :] + last
    wide = jnp.concatenate([total, jnp.zeros((1, 128 - heads), F32)], axis=1)
    total_ref[...] = jnp.broadcast_to(wide, (8, 128))


def diag_pieces(x_ref, bc_ref, step_ref, cum_ref, skip, y_ref):
    rows, heads = step_ref.shape
    n = bc_ref.shape[1] // 2
    half = GROUP // 2
    zero = jnp.zeros((), BF16)

    def piece(b, pairs):
        r = pl.ds(b * GROUP, GROUP)
        eye = (iota((heads, heads), 0) == iota((heads, heads), 1)).astype(F32)
        left = iota((GROUP, 2 * CH), 1) < CH
        gains = spread(jnp.broadcast_to(skip, (8, heads)), heads)[0:1]
        scores = bdot(bc_ref[r, n:], bc_ref[r, :n], NT)
        scores = jnp.where(lower(GROUP), scores, 0.0)
        cum = cum_ref[r, :]
        cum_row = exact_dot(eye, cum, NT)
        step_row = exact_dot(eye, step_ref[r, :], NT)
        for pair in pairs:
            lanes = pl.ds(pair * 2 * CH, 2 * CH)
            xp = x_ref[r, lanes]
            tops, bottoms = [], []
            for side in range(2):
                h = 2 * pair + side
                mine = jnp.where(left if side == 0 else ~left, xp, zero)
                col = cum[:, h : h + 1]
                row = cum_row[h : h + 1, :]
                srow = step_row[h : h + 1, :]
                top = (
                    jnp.exp(jnp.minimum(col[:half] - row[:, :half], 0.0))
                    * scores[:half, :half]
                    * srow[:, :half]
                ).astype(BF16)
                bottom = (
                    jnp.exp(jnp.minimum(col[half:] - row, 0.0)) * scores[half:, :] * srow
                ).astype(BF16)
                tops.append(bdot(top, mine[:half]))
                bottoms.append(bdot(bottom, mine))
            xs = xp.astype(F32) * gains[:, pair * 2 * CH : (pair + 1) * 2 * CH]
            y_ref[pl.ds(b * GROUP, half), lanes] = tops[0] + tops[1] + xs[:half]
            y_ref[pl.ds(b * GROUP + half, half), lanes] = bottoms[0] + bottoms[1] + xs[half:]

    quarter = heads // 4
    return [
        functools.partial(piece, b, range(k * quarter, (k + 1) * quarter))
        for b in range(rows // GROUP)
        for k in range(2)
    ]


def mixed_blocks(bc_ref, cum_ref, prev_ref, st_ref, y_ref):
    rows, heads = cum_ref.shape
    n = bc_ref.shape[1] // 2
    out = []
    high = None
    for b in range(rows // GROUP):
        r = pl.ds(b * GROUP, GROUP)
        c = bc_ref[r, n:]
        cum = cum_ref[r, :]
        if b == 0:
            high = prev_ref[...]
            inner = bdot(c, high)
        else:
            last = cum_ref[pl.ds(GROUP - 8, 8), :]
            factor = spread(jnp.exp(last), heads)[7:8]
            state = factor * high.astype(F32) + st_ref[...]
            hi, lo = split_two(state)
            inner = bdot(c, hi) + bdot(c, lo)
        out.append((r, y_ref[r, :] + inner * spread(jnp.exp(cum), heads)))
    return out


def squares(v):
    sq = v * v
    part = sum(sq[:, k : k + 128] for k in range(128, v.shape[1], 128)) + sq[:, :128]
    return exact_dot(jnp.ones((8, 128), F32), part, NT)


def gate_body(bc_ref, cum_ref, prev_ref, st_ref, y_ref, gate_ref, gain, g_ref, ss_ref):
    for r, mixed in mixed_blocks(bc_ref, cum_ref, prev_ref, st_ref, y_ref):
        gate = gate_ref[r, :].astype(F32)
        gated = mixed * (gate / (1.0 + jnp.exp(-gate)))
        g_ref[r, :] = (gated * gain).astype(BF16)
        ss_ref[:, r] = squares(gated)


def last_body(bc_ref, cum_ref, prev_ref, st_ref, y_ref, m_ref, ss_ref):
    for r, mixed in mixed_blocks(bc_ref, cum_ref, prev_ref, st_ref, y_ref):
        m_ref[r, :] = mixed
        ss_ref[:, r] = squares(mixed)


NC = 8
CHUNK_LAG = 2
MESH = pl.DeviceIdType.MESH
Y, Z, CORES = 4, 8, 2


def place():
    seq = lax.axis_index("seq")
    return seq // (Z * CORES), (seq // CORES) % Z, seq % CORES


def seq_of(y, z, c):
    return (y * Z + z) * CORES + c


class Copies:
    def __init__(self, send_sem, recv_sem):
        self.send_sem, self.recv_sem = send_sem, recv_sem
        self.names = {}
        self.started = []

    def _make(self, name, src, dst, device):
        at = self.names.setdefault(name, len(self.names))
        return pltpu.make_async_remote_copy(
            src_ref=src, dst_ref=dst, send_sem=self.send_sem.at[at], recv_sem=self.recv_sem.at[at],
            device_id=device, device_id_type=MESH,
        )

    def send(self, name, src, dst, device):
        copy = self._make(name, src, dst, device)
        copy.start()
        self.started.append(copy)

    def arrived(self, name, where, device):
        self._make(name, where, where, device).wait_recv()

    def finish(self):
        for copy in self.started:
            copy.wait_send()


def weight_steps(cp, tag, own, w, local_sem, a_rows):
    y, z, c = place()
    head = lax.axis_index("head")
    f = 1 - 2 * c
    top, low = pl.ds(0, a_rows), pl.ds(a_rows, own.shape[0] - a_rows)

    def at_y(k):
        return lax.rem(y + k * f + 2 * Y, Y)

    def at_z(k):
        return lax.rem(z + k * f + 2 * Z, Z)

    to_y = {k: (seq_of(at_y(k), z, c), head) for k in (1, -1)}
    to_z = {k: (seq_of(y, at_z(k), c), head) for k in (1, -1)}
    other = (seq_of(y, z, 1 - c), head)

    def a_piece(ky):
        return w.at[at_y(ky), z, c, top]

    def a_block(kz):
        return w.at[:, at_z(kz), c, top]

    def b_piece(ky, kz):
        return w.at[at_y(ky), at_z(kz), c, low]

    def push(name, ref, device):
        cp.send((tag, *name), ref, ref, device)

    def here(name, ref, device):
        cp.arrived((tag, *name), ref, device)

    def a_share(kz):
        push(("as", kz), a_block(kz), other)

    def b_share(ky, kz):
        push(("bs", ky, kz), b_piece(ky, kz), other)

    def a_went(way, k):
        kz = -way * (k + 1)
        here(("az", way, k), a_block(kz), to_z[way])
        if k < (3 if way == 1 else 2):
            push(("az", way, k + 1), a_block(kz), to_z[way])
        a_share(kz)

    def b_went(way, k):
        kz = -way * (k + 1)
        here(("bz", way, k), b_piece(0, kz), to_z[way])
        if k < (3 if way == -1 else 2):
            push(("bz", way, k + 1), b_piece(0, kz), to_z[way])
        for along in (-1, 1):
            push(("by", along, kz), b_piece(0, kz), to_y[along])
        b_share(0, kz)

    def b_on(kz):
        here(("by", -1, kz), b_piece(1, kz), to_y[-1])
        push(("bf", kz), b_piece(1, kz), to_y[-1])
        b_share(1, kz)
        here(("by", 1, kz), b_piece(-1, kz), to_y[1])
        b_share(-1, kz)

    def b_end(kz):
        here(("bf", kz), b_piece(2, kz), to_y[-1])
        b_share(2, kz)

    def s0():
        mine = pltpu.make_async_copy(own, w.at[y, z, c], local_sem)
        mine.start()
        for way in (1, -1):
            cp.send((tag, "ay", way, 0), own.at[top], a_piece(0), to_y[way])
            cp.send((tag, "bz", way, 0), own.at[low], b_piece(0, 0), to_z[way])
        for way in (-1, 1):
            cp.send((tag, "by", way, 0), own.at[low], b_piece(0, 0), to_y[way])
        mine.wait()

    def s1():
        here(("ay", 1, 0), a_piece(-1), to_y[1])
        push(("ay", 1, 1), a_piece(-1), to_y[1])
        b_went(1, 0)
        b_went(-1, 0)

    def s2():
        b_went(1, 1)
        b_went(-1, 1)
        here(("ay", -1, 0), a_piece(1), to_y[-1])
        here(("ay", 1, 1), a_piece(-2), to_y[1])
        for way in (1, -1):
            push(("az", way, 0), a_block(0), to_z[way])
        b_on(0)
        a_share(0)
        b_share(0, 0)

    def s3():
        b_went(1, 2)
        b_went(-1, 2)
        b_on(-1)
        b_on(1)
        a_went(1, 0)
        a_went(-1, 0)

    def s4():
        b_went(-1, 3)
        b_on(-2)
        b_on(2)
        a_went(1, 1)
        a_went(-1, 1)
        b_end(0)

    def s5():
        b_on(-3)
        b_on(3)
        a_went(1, 2)
        a_went(-1, 2)
        b_end(-1)
        b_end(1)

    def s6():
        b_on(4)
        a_went(1, 3)
        b_end(-2)
        b_end(2)

    def s7():
        for kz in (-3, 3, 4):
            b_end(kz)

    def s8():
        for kz in range(-4, 4):
            here(("as", kz), w.at[:, lax.rem(z - kz * f + 2 * Z, Z), 1 - c, top], other)
        for ky in range(-1, 3):
            for kz in range(-3, 5):
                where = w.at[lax.rem(y - ky * f + 2 * Y, Y), lax.rem(z - kz * f + 2 * Z, Z), 1 - c, low]
                here(("bs", ky, kz), where, other)

    return [s0, s1, s2, s3, s4, s5, s6, s7, s8]


def prefix_steps(cp, tag, heads, end_ref, total_ref, prev_ref, p):
    y, z, c = place()
    head = lax.axis_index("head")
    other = (seq_of(y, z, 1 - c), head)
    n, width = end_ref.shape
    half, lanes, part = n // 2, width // 2, heads // 2
    to_z = {k: (seq_of(y, lax.rem(z + k, Z), c), head) for k in range(1, Z)}
    to_y = {k: (seq_of(lax.rem(y + k, Y), z, c), head) for k in range(1, Y)}
    mine = pl.ds(pl.multiple_of(c * half, half), half)
    theirs = pl.ds(pl.multiple_of((1 - c) * half, half), half)
    first = c == 0

    def cell(j):
        return pl.ds((j // 2) * 16, 16), pl.ds((j % 2) * lanes, lanes)

    def factor(log):
        return spread(jnp.exp(log), part)

    def log_of(tail):
        return tail[:, :part] + tail[:, part : 2 * part] + tail[:, 2 * part : 3 * part]

    def core_out():
        p.pair_out[pl.ds(0, half), :] = end_ref[theirs, :]
        p.pair_out[pl.ds(half, 8), pl.ds(0, 128)] = total_ref[...]
        p.pair_out[pl.ds(half, 8), pl.ds(128, width - 128)] = jnp.zeros((8, width - 128), F32)
        cp.send((tag, "out"), p.pair_out, p.pair_in, other)

    def z_out():
        cp.arrived((tag, "out"), p.pair_in, other)
        own, got = end_ref[mine, :], p.pair_in[pl.ds(0, half), :]
        own_log = total_ref[:, :heads]
        got_log = p.pair_in[pl.ds(half, 8), pl.ds(0, 128)][:, :heads]
        s0, s1 = jnp.where(first, own, got), jnp.where(first, got, own)
        log0, log1 = jnp.where(first, own_log, got_log), jnp.where(first, got_log, own_log)
        p.zero_state[...] = s0
        p.zero_factor[...] = spread(jnp.exp(log0), heads)
        chip = spread(jnp.exp(log1), heads)[0:1] * s0 + s1
        log = log0 + log1
        log = jnp.concatenate([log, log], axis=0)
        for j in range(Z):
            r, q = cell(j)
            p.z_out[j, :, pl.ds(0, lanes)] = chip[r.start : r.start + 16, q.start : q.start + lanes].astype(BF16)
            rest = log[:, (j % 2) * part : (j % 2 + 1) * part]
            pieces = []
            for _ in range(3):
                piece = rest.astype(BF16).astype(F32)
                pieces.append(piece)
                rest = rest - piece
            pieces.append(jnp.zeros((16, 128 - 3 * part), F32))
            p.z_out[j, :, pl.ds(lanes, 128)] = jnp.concatenate(pieces, axis=1).astype(BF16)
        for k in FAR_FIRST:
            cp.send((tag, "z", k), p.z_out.at[lax.rem(z + k, Z)], p.z_in.at[z], to_z[k])
        p.z_in[z] = p.z_out[z]

    def y_out():
        for k in range(1, Z):
            cp.arrived((tag, "z", k), p.z_in.at[lax.rem(z - k + Z, Z)], to_z[k])
        run = jnp.zeros((16, lanes), F32)
        logs = jnp.zeros((16, part), F32)
        every = log_of(p.z_in[:, :, pl.ds(lanes, 128)].astype(F32).reshape(Z * 16, 128))
        factors = factor(every)
        for j in range(Z):
            log, f = every[16 * j : 16 * j + 16], factors[16 * j : 16 * j + 16]
            p.z_factor[j] = f
            run = f * run + p.z_in[j, :, pl.ds(0, lanes)].astype(F32)
            logs = logs + log
        p.y_in[y, :, pl.ds(0, lanes)] = run
        p.y_in[y, :, pl.ds(lanes, 128)] = jnp.concatenate([logs, jnp.zeros((16, 128 - part), F32)], axis=1)
        for k in range(1, Y):
            cp.send((tag, "y", k), p.y_in.at[y], p.y_in.at[y], to_y[k])

    def z_back():
        for k in range(1, Y):
            cp.arrived((tag, "y", k), p.y_in.at[lax.rem(y - k + Y, Y)], to_y[k])
        run = jnp.zeros((16, lanes), F32)
        factors = factor(p.y_in[:, :, pl.ds(lanes, 128)].reshape(Y * 16, 128)[:, :part])
        for j in range(Y):
            f = factors[16 * j : 16 * j + 16]
            run = jnp.where(j < y, f * run + p.y_in[j, :, pl.ds(0, lanes)], run)
        for j in range(Z):
            p.back_out[j] = run.astype(BF16)
            run = p.z_factor[j] * run + p.z_in[j, :, pl.ds(0, lanes)].astype(F32)
        for k in FAR_FIRST:
            cp.send((tag, "b", k), p.back_out.at[lax.rem(z + k, Z)], p.back_in.at[z], to_z[k])
        p.back_in[z] = p.back_out[z]

    def core_back():
        for k in range(1, Z):
            cp.arrived((tag, "b", k), p.back_in.at[lax.rem(z - k + Z, Z)], to_z[k])
        rows = [
            jnp.concatenate([p.back_in[2 * i], p.back_in[2 * i + 1]], axis=1) for i in range(Z // 2)
        ]
        zero = jnp.concatenate(rows, axis=0).astype(F32)
        one = p.zero_factor[0:1, :] * zero + p.zero_state[...]
        p.core_out[...] = jnp.where(first, one, zero).astype(BF16)
        cp.send((tag, "core"), p.core_out, prev_ref.at[mine], other)
        prev_ref[mine, :] = jnp.where(first, zero, one).astype(BF16)

    def done():
        cp.arrived((tag, "core"), prev_ref.at[theirs], other)

    return [core_out, z_out, y_out, z_back, core_back, done], [*to_z.values(), *to_y.values(), other]


FAR_FIRST = sorted(range(1, Z), key=lambda k: -min(k, Z - k))
N_PREFIX_COPIES = 2 * Z + Y - 1


N_WEIGHT_COPIES = 53 + 28


def greet(devices):
    barrier = pltpu.get_barrier_semaphore()
    for device in devices:
        pl.semaphore_signal(barrier, inc=1, device_id=device, device_id_type=MESH)
    pl.semaphore_wait(barrier, len(devices))


def mixer_body(names, *refs):
    a = types.SimpleNamespace(**dict(zip(names, refs)))
    rows, width = a.x_in.shape
    heads = a.step_in.shape[0]
    states = a.bc_in.shape[1]
    seq, me = lax.axis_index("seq"), lax.axis_index("head")
    n_seq, n_head = lax.axis_size("seq"), lax.axis_size("head")
    depth = width * n_head
    r, o, l = (lax.rem(me + k, n_head) for k in (1, 2, 3))
    right, opposite, left = ((seq, k) for k in (r, o, l))
    after, before = ((lax.rem(seq + k, n_seq), me) for k in (1, n_seq - 1))
    across = ((1, right), (2, opposite), (3, left))
    cp = Copies(a.send_sem, a.recv_sem)
    out_steps = weight_steps(cp, "wo", a.w_out, a.wo, a.local_sem.at[0], 16)
    steps = weight_steps(cp, "wi", a.wi_own, a.wi, a.local_sem.at[1], 32)

    def prefix_of(layer):
        views = {k: getattr(a, k).at[layer] for k in PREFIX_NAMES}
        return prefix_steps(
            cp, ("prefix", layer), heads, a.end, a.total, a.prev.at[layer], types.SimpleNamespace(**views)
        )

    prefix, partners = prefix_of(0)
    loads = {
        name: pltpu.make_async_copy(getattr(a, name + "_hbm"), getattr(a, name), a.local_sem.at[2 + k])
        for k, name in enumerate(LATE)
    }
    for load in loads.values():
        load.start()
    a.wi_own[:, pl.ds(0, width)] = a.w_in_x[...]
    a.wi_own[:, pl.ds(width, states)] = a.w_in_bc[...]
    dt = a.w_in_dt[...].astype(F32).T
    dt = jnp.concatenate([dt, jnp.zeros((dt.shape[0], 128 - heads), F32)], axis=1)
    a.wi_own[:, pl.ds(width + states, 128)] = dt.astype(BF16)
    a.step_one[...] = a.step_in[...].T
    greet([right, opposite, left, after, before, *partners])

    def turn(work):
        if work:
            work.pop(0)()

    turn(out_steps)
    loads["x_in"].wait()
    loads["bc_in"].wait()

    def block_states(layer, b, x_ref, bc_ref, step_ref):
        code = a.code[layer, :, b * GROUP : (b + 1) * GROUP]
        rate = a.rate[layer : layer + 1, :]
        states_block(b, x_ref, bc_ref, step_ref, code, rate, a.st, a.end, a.total, a.cum)

    for b in range(rows // GROUP):
        block_states(0, b, a.x_in, a.bc_in, a.step_one)
    turn(prefix)
    turn(out_steps)
    diag = diag_pieces(a.x_in, a.bc_in, a.step_one, a.cum, a.skip[0:1, :], a.own)
    while prefix:
        turn(diag)
        turn(prefix)
        turn(out_steps)
    loads["gate"].wait()
    loads["resid_in"].wait()
    gate_body(a.bc_in, a.cum, a.prev.at[0], a.st, a.own, a.gate, a.norm_gain[...], a.g, a.ss.at[0])
    for k, device in across:
        cp.send(("ss", k), a.ss.at[0], a.ss_in.at[k - 1], device)
    while len(out_steps) > 1:
        turn(out_steps)
    turn(steps)
    turn(out_steps)

    g_ref, wo_ref, resid_ref, gain_ref, bias_ref = a.g, a.wo, a.resid_in, a.resid_gain, a.bias
    cx_ref, cbc_ref, out_ref, x_ref, bc_ref, step_ref = a.conv_x, a.conv_bc, a.resid_out, a.x_two, a.bc_two, a.step_two
    w_ref, hid_ref, h_ref, opp_ref, right_ref, left_ref, own_ref = a.wi, a.hid, a.h, a.opp, a.right, a.left, a.own
    sum_r_ref, sum_l_ref, in_l1, in_r1, in_l2, in_r2 = a.sum_r, a.sum_l, a.in_l1, a.in_r1, a.in_l2, a.in_r2
    ss_ref, ss_in, tail_ref, halo_ref, scale_ref, rs_ref, pre_ref = (
        a.ss.at[0], a.ss_in, a.tail, a.halo, a.scale, a.rs, a.pre
    )
    chunk = rows // NC
    half = width // 2
    lo, hi = pl.ds(0, half), pl.ds(half, half)
    order = [NC - 1, *range(NC - 1)]
    tile = 256

    def cut(c):
        return pl.ds(c * chunk, chunk)

    def product(dest, store):
        @pl.loop(0, width // tile)
        def _(j):
            at = pl.multiple_of(j * tile, tile)
            weight = wo_ref[dest, pl.ds(j * (Z // 4), Z // 4)].reshape(tile, width)
            store(pl.ds(at, tile), bdot(g_ref[...], weight, NT))

    def project():
        def to_opp(cols, p):
            opp_ref[:, cols] = p.astype(BF16)

        def keep(ref):
            def store(cols, p):
                ref[:, cols] = p

            return store

        product(o, to_opp)
        for c in order:
            cp.send(("1r", c), opp_ref.at[cut(c), lo], in_l1.at[cut(c)], right)
            cp.send(("1l", c), opp_ref.at[cut(c), hi], in_r1.at[cut(c)], left)
        product(r, keep(right_ref))
        product(l, keep(left_ref))
        product(me, keep(own_ref))

    def second_sum(c):
        q = cut(c)
        cp.arrived(("1r", c), in_l1.at[q], right)
        sum_r_ref[q, lo] = (right_ref[q, lo] + in_l1[q, :].astype(F32)).astype(BF16)
        sum_r_ref[q, hi] = right_ref[q, hi].astype(BF16)
        cp.send(("2r", c), sum_r_ref.at[q], in_l2.at[q], right)
        cp.arrived(("1l", c), in_r1.at[q], left)
        sum_l_ref[q, hi] = (left_ref[q, hi] + in_r1[q, :].astype(F32)).astype(BF16)
        sum_l_ref[q, lo] = left_ref[q, lo].astype(BF16)
        cp.send(("2l", c), sum_l_ref.at[q], in_r2.at[q], left)

    def token_scale(tag, ss_ref, ss_in):
        for k, device in across:
            cp.arrived((tag, k), ss_in.at[k - 1], device)
        total = ss_ref[...] + ss_in[0] + ss_in[1] + ss_in[2]
        eighth = jnp.full((8, 128), 0.125, F32)
        column = exact_dot(total, eighth, (((0,), (0,)), ((), ())))
        scale_ref[...] = lax.rsqrt(column / depth + 1e-05)

    def residual(c):
        q = cut(c)
        cp.arrived(("2r", c), in_l2.at[q], right)
        cp.arrived(("2l", c), in_r2.at[q], left)
        total = own_ref[q, :] + in_l2[q, :].astype(F32) + in_r2[q, :].astype(F32)
        total = total * scale_ref[q, 0:1] + resid_ref[q, :].astype(F32)
        out_ref[q, :] = total.astype(BF16)
        hid_ref[me, q, :] = out_ref[q, :]
        cp.send(("3r", c), hid_ref.at[me, q], hid_ref.at[me, q], right)
        cp.send(("3l", c), hid_ref.at[me, q], hid_ref.at[me, q], left)

    def hand_on(c):
        q = cut(c)
        cp.arrived(("3r", c), hid_ref.at[l, q], right)
        cp.send(("4r", c), hid_ref.at[l, q, lo], hid_ref.at[l, q, lo], right)
        cp.arrived(("3l", c), hid_ref.at[r, q], left)
        cp.send(("4l", c), hid_ref.at[r, q, hi], hid_ref.at[r, q, hi], left)

    def scaled(src, q, at, n, keep):
        parts = [src[k, q, :].astype(F32) for k in range(n_head)]
        total = sum(jnp.sum(v * v, axis=1, keepdims=True) for v in parts)
        rs = lax.rsqrt(total / depth + 1e-05)
        rs_ref[pl.ds(at, n), :] = jnp.broadcast_to(rs if keep is None else rs * keep, (n, 128))
        for k, v in enumerate(parts):
            h_ref[k, pl.ds(at, n), :] = (v * gain_ref[:, k * width : (k + 1) * width]).astype(BF16)

    def complete(c):
        q = cut(c)
        cp.arrived(("4r", c), hid_ref.at[o, q, lo], right)
        cp.arrived(("4l", c), hid_ref.at[o, q, hi], left)
        if c == NC - 1:
            tail_ref[...] = hid_ref[:, pl.ds(rows - HALO, HALO), :]
            cp.send("halo", tail_ref, halo_ref, after)
        scaled(hid_ref, q, c * chunk + HALO, chunk, None)

    def into(cols, at, n):
        total = None
        for k in range(n_head):
            piece = bdot(
                h_ref[k, pl.ds(at, n), :], w_ref[k, :, :, :, cols].reshape(width, cols.size)
            )
            total = piece if total is None else total + piece
        return total

    def conv(taps, k):
        n = taps.shape[1]
        total = None
        for tap in range(k):
            v = pre_ref[pl.ds(HALO - k + 1 + tap, GROUP), :n] * taps[tap : tap + 1, :].astype(F32)
            total = v if total is None else total + v
        return (total / (1.0 + jnp.exp(-total))).astype(BF16)

    def second_inputs(b):
        at, every = b * GROUP, GROUP + HALO
        r = pl.ds(at, GROUP)

        def pre(cols):
            rs = rs_ref[pl.ds(at, every), :]
            both = jnp.concatenate([rs, rs], axis=1)
            pre_ref[...] = (into(cols, at, every) * both).astype(BF16).astype(F32)

        @pl.loop(0, width // tile)
        def _(i):
            cols = pl.ds(pl.multiple_of(i * tile, tile), tile)
            pre(cols)
            x_ref[r, cols] = conv(cx_ref[:, cols], cx_ref.shape[0])

        pre(pl.ds(width, states))
        bc_ref[r, :] = conv(cbc_ref[...], cbc_ref.shape[0])
        dt = into(pl.ds(width + states, 128), at + HALO, GROUP)
        dt = (dt * rs_ref[pl.ds(at + HALO, GROUP), :])[:, :heads] + bias_ref[...]
        step_ref[r, :] = jnp.maximum(dt, 0.0) + jnp.log(1.0 + jnp.exp(-jnp.abs(dt)))

    diag = diag_pieces(x_ref, bc_ref, step_ref, a.cum, a.skip[1:2, :], a.right)

    def first_block(t):
        if t == 4 + 3 * CHUNK_LAG:
            cp.arrived("halo", halo_ref, after)
            scaled(halo_ref, pl.ds(0, HALO), 0, HALO, jnp.where(seq == 0, 0.0, 1.0))
            while steps:
                turn(steps)
            second_inputs(0)
        if t == 5 + 3 * CHUNK_LAG:
            block_states(1, 0, x_ref, bc_ref, step_ref)
        if t >= 6 + 3 * CHUNK_LAG:
            turn(diag)

    project()
    for t in range(NC + 3 * CHUNK_LAG):
        for stage, work in reversed(list(enumerate((second_sum, residual, hand_on, complete)))):
            k = t - CHUNK_LAG * stage
            if 0 <= k < NC:
                if work is residual and k == 0:
                    token_scale("ss", ss_ref, ss_in)
                work(order[k])
        if t >= 1:
            turn(steps)
        first_block(t)
    second_inputs(1)
    block_states(1, 1, x_ref, bc_ref, step_ref)
    prefix, _ = prefix_of(1)
    turn(prefix)
    while prefix:
        turn(diag)
        turn(prefix)
    last_body(bc_ref, a.cum, a.prev.at[1], a.st, a.right, a.left, a.ss.at[1])
    for k, device in across:
        cp.send(("ss two", k), a.ss.at[1], a.ss_two.at[k - 1], device)
    token_scale("ss two", a.ss.at[1], a.ss_two)
    for c in range(NC):
        q = cut(c)
        a.mixer_out[q, :] = (a.left[q, :] * scale_ref[q, 0:1]).astype(BF16)
    cp.finish()


PARTS = 8


def place_body(one_ref, two_ref, one_out, two_out, sem):
    step = one_ref.shape[0] // PARTS
    copies = [
        pltpu.make_async_copy(src.at[pl.ds(k * step, step)], dst.at[pl.ds(k * step, step)], sem.at[i, k])
        for k in range(PARTS)
        for i, (src, dst) in enumerate(((one_ref, one_out), (two_ref, two_out)))
    ]
    for copy in copies:
        copy.start()
    for copy in copies:
        copy.wait()


LATE = ("x_in", "bc_in", "gate", "resid_in")
PREFIX_NAMES = (
    "pair_out", "pair_in", "zero_state", "zero_factor", "z_out", "z_in", "z_factor", "y_in", "back_out", "back_in", "core_out",
)


def mixer(ins, rows, width, heads, states):
    n_head = lax.axis_size("head")
    n = states // 2
    lanes = width // 2
    copies = 2 * N_WEIGHT_COPIES + 2 * N_PREFIX_COPIES + 6 + 1 + 8 * NC
    outs = {"resid_out": sds(rows, width, dtype=BF16), "mixer_out": sds(rows, width, dtype=BF16)}

    def keep(*shape, dtype=F32):
        return pltpu.VMEM(shape, dtype)

    small = functools.partial(keep, dtype=BF16)
    scratch = {
        "wo": small(Y, Z, CORES, *ins["w_out"].shape),
        "wi": small(Y, Z, CORES, ins["w_in_x"].shape[0], width + states + 128),
        "hid": small(n_head, rows, width),
        "h": small(n_head, rows + HALO, width),
        "opp": small(rows, width),
        "right": keep(rows, width),
        "left": keep(rows, width),
        "own": keep(rows, width),
        "sum_r": small(rows, width),
        "sum_l": small(rows, width),
        "in_l1": small(rows, lanes),
        "in_r1": small(rows, lanes),
        "in_l2": small(rows, width),
        "in_r2": small(rows, width),
        "g": small(rows, width),
        "x_two": small(rows, width),
        "bc_two": small(rows, states),
        "step_two": keep(rows, heads),
        "cum": keep(rows, heads),
        "st": keep(n, width),
        "end": keep(n, width),
        "total": keep(8, 128),
        "prev": small(2, n, width),
        "ss": keep(2, 8, rows),
        "ss_in": keep(3, 8, rows),
        "ss_two": keep(3, 8, rows),
        "tail": small(n_head, HALO, width),
        "halo": small(n_head, HALO, width),
        "scale": keep(rows, 128),
        "rs": keep(rows + HALO, 128),
        "pre": keep(GROUP + HALO, 256),
        "wi_own": small(ins["w_in_x"].shape[0], width + states + 128),
        **{name: small(*ins[name + "_hbm"].shape) for name in LATE},
        "step_one": keep(rows, heads),
        "pair_out": keep(2, n // 2 + 8, width),
        "pair_in": keep(2, n // 2 + 8, width),
        "zero_state": keep(2, n // 2, width),
        "zero_factor": keep(2, 8, width),
        "z_out": small(2, Z, 16, lanes + 128),
        "z_in": small(2, Z, 16, lanes + 128),
        "z_factor": keep(2, Z, 16, lanes),
        "y_in": keep(2, Y, 16, lanes + 128),
        "back_out": small(2, Z, 16, lanes),
        "back_in": small(2, Z, 16, lanes),
        "core_out": small(2, n // 2, width),
        "send_sem": pltpu.SemaphoreType.DMA((copies,)),
        "recv_sem": pltpu.SemaphoreType.DMA((copies,)),
        "local_sem": pltpu.SemaphoreType.DMA((2 + len(LATE),)),
    }
    return call(
        functools.partial(mixer_body, (*ins, *outs, *scratch)),
        tuple(outs.values()),
        tuple(ins.values()),
        scratch.values(),
        limit=58,
        far=[name.endswith("_hbm") for name in ins],
        collective_id=1,
        has_side_effects=True,
    )


def call(body, outs, args, scratch=(), limit=56, far=(), **kw):
    return pl.pallas_call(
        body,
        out_shape=outs,
        in_specs=[pl.BlockSpec(memory_space=pl.ANY) if k else VMEM for k in far],
        out_specs=jax.tree.map(lambda _: VMEM, outs),
        scratch_shapes=list(scratch),
        compiler_params=pltpu.CompilerParams(vmem_limit_bytes=limit * 2**20, **kw),
    )(*args)


def sds(*shape, dtype=F32):
    return jax.ShapeDtypeStruct(shape, dtype)


def on_device(
    x_in, gate_in, bc_in, step_in, decay_code, decay_rate, skip_gain, norm_gain, w_out, resid_in,
    resid_gain, w_in_x, w_in_bc, w_in_dt, step_time_bias, conv_x, conv_bc,
):
    rows, width = x_in.shape
    heads = step_in.shape[1]
    ins = {
        "x_in_hbm": x_in, "gate_hbm": gate_in, "bc_in_hbm": bc_in, "step_in": step_in.T, "code": jnp.swapaxes(decay_code, 1, 2), "rate": decay_rate,
        "skip": skip_gain, "norm_gain": norm_gain[None, :], "w_out": w_out.T, "resid_in_hbm": resid_in,
        "resid_gain": resid_gain[None, :], "w_in_x": w_in_x, "w_in_bc": w_in_bc, "w_in_dt": w_in_dt.T, "bias": step_time_bias[None, :], "conv_x": conv_x,
        "conv_bc": conv_bc,
    }
    outs = mixer(ins, rows, width, heads, bc_in.shape[1])
    anywhere = pl.BlockSpec(memory_space=pl.ANY)
    return pl.pallas_call(
        place_body,
        out_shape=tuple(sds(*v.shape, dtype=v.dtype) for v in outs),
        in_specs=[anywhere] * 2,
        out_specs=(anywhere,) * 2,
        scratch_shapes=[pltpu.SemaphoreType.DMA((2, PARTS))],
        compiler_params=pltpu.CompilerParams(vmem_limit_bytes=2**20),
    )(*outs)


def solution(mesh):
    in_specs = (
        P("seq", "head"), P("seq", "head"), P("seq", None), P("seq", "head"), P(None, "seq", "head"),
        P(None, "head"), P(None, "head"), P("head"), P("head", "seq"), P("seq", "head"), P(),
        P("seq", "head"), P("seq", None), P("seq", "head"), P("head"), P(None, "head"), P(),
    )
    out_specs = (P("seq", "head"), P("seq", "head"))
    return jax.shard_map(
        on_device, mesh=mesh, in_specs=in_specs, out_specs=out_specs, check_vma=False
    )
```

```python
import functools
import types

import jax
import jax.numpy as jnp
from jax import lax
from jax.experimental import pallas as pl
from jax.experimental.pallas import tpu as pltpu
from jax.sharding import PartitionSpec as P

CH = 64
GROUP = 256
F32 = jnp.float32
BF16 = jnp.bfloat16
NT = (((1,), (1,)), ((), ()))
VMEM = pl.BlockSpec(memory_space=pltpu.VMEM)
HALO = 16


def iota(shape, dim):
    return lax.broadcasted_iota(jnp.int32, shape, dim)


def exact_dot(a, b, dims=None):
    if dims is None:
        return jnp.dot(a, b, precision=lax.Precision.HIGHEST, preferred_element_type=F32)
    return lax.dot_general(a, b, dims, precision=lax.Precision.HIGHEST, preferred_element_type=F32)


def bdot(a, b, dims=None):
    if dims is None:
        return jnp.dot(a, b, preferred_element_type=F32)
    return lax.dot_general(a, b, dims, preferred_element_type=F32)


def split_two(v):
    hi = v.astype(BF16)
    return hi, (v - hi.astype(F32)).astype(BF16)


def spread(v, heads):
    width = heads * CH
    e = (iota((heads, width), 1) // CH == iota((heads, width), 0)).astype(BF16)
    hi, lo = split_two(v)
    return bdot(hi, e) + bdot(lo, e)


def lower(n):
    return iota((n, n), 0) >= iota((n, n), 1)


def states_block(b, x_ref, bc_ref, step_ref, code, rate, st_ref, end_ref, total_ref, cum_ref):
    heads = step_ref.shape[1]
    r = pl.ds(b * GROUP, GROUP)
    decay = -jnp.minimum(code.astype(F32).T * rate, 20.0)
    cum = exact_dot(lower(GROUP).astype(F32), decay)
    cum_ref[r, :] = cum
    last = cum[GROUP - 1 : GROUP, :]
    weight = jnp.exp(last - cum) * step_ref[r, :]
    v = (x_ref[r, :].astype(F32) * spread(weight, heads)).astype(BF16)
    term = lax.dot_general(
        bc_ref[r, : bc_ref.shape[1] // 2], v, (((0,), (0,)), ((), ())), preferred_element_type=F32
    )
    if b == 0:
        st_ref[...] = term
        return
    factor = spread(jnp.broadcast_to(jnp.exp(last), (8, heads)), heads)[0:1]
    end_ref[...] = factor * st_ref[...] + term
    total = cum_ref[pl.ds(GROUP - 1, 1), :] + last
    wide = jnp.concatenate([total, jnp.zeros((1, 128 - heads), F32)], axis=1)
    total_ref[...] = jnp.broadcast_to(wide, (8, 128))


def diag_pieces(x_ref, bc_ref, step_ref, cum_ref, skip, y_ref):
    rows, heads = step_ref.shape
    n = bc_ref.shape[1] // 2
    half = GROUP // 2
    zero = jnp.zeros((), BF16)

    def piece(b, pairs):
        r = pl.ds(b * GROUP, GROUP)
        eye = (iota((heads, heads), 0) == iota((heads, heads), 1)).astype(F32)
        left = iota((GROUP, 2 * CH), 1) < CH
        gains = spread(jnp.broadcast_to(skip, (8, heads)), heads)[0:1]
        scores = bdot(bc_ref[r, n:], bc_ref[r, :n], NT)
        scores = jnp.where(lower(GROUP), scores, 0.0)
        cum = cum_ref[r, :]
        cum_row = exact_dot(eye, cum, NT)
        step_row = exact_dot(eye, step_ref[r, :], NT)
        for pair in pairs:
            lanes = pl.ds(pair * 2 * CH, 2 * CH)
            xp = x_ref[r, lanes]
            tops, bottoms = [], []
            for side in range(2):
                h = 2 * pair + side
                mine = jnp.where(left if side == 0 else ~left, xp, zero)
                col = cum[:, h : h + 1]
                row = cum_row[h : h + 1, :]
                srow = step_row[h : h + 1, :]
                top = (
                    jnp.exp(jnp.minimum(col[:half] - row[:, :half], 0.0))
                    * scores[:half, :half]
                    * srow[:, :half]
                ).astype(BF16)
                bottom = (
                    jnp.exp(jnp.minimum(col[half:] - row, 0.0)) * scores[half:, :] * srow
                ).astype(BF16)
                tops.append(bdot(top, mine[:half]))
                bottoms.append(bdot(bottom, mine))
            xs = xp.astype(F32) * gains[:, pair * 2 * CH : (pair + 1) * 2 * CH]
            y_ref[pl.ds(b * GROUP, half), lanes] = tops[0] + tops[1] + xs[:half]
            y_ref[pl.ds(b * GROUP + half, half), lanes] = bottoms[0] + bottoms[1] + xs[half:]

    quarter = heads // 4
    return [
        functools.partial(piece, b, range(k * quarter, (k + 1) * quarter))
        for b in range(rows // GROUP)
        for k in range(2)
    ]


def mixed_blocks(bc_ref, cum_ref, prev_ref, st_ref, y_ref, grown_ref):
    rows, heads = cum_ref.shape
    n = bc_ref.shape[1] // 2
    out = []
    high = None
    for b in range(rows // GROUP):
        r = pl.ds(b * GROUP, GROUP)
        c = bc_ref[r, n:]
        if b == 0:
            high = prev_ref[...]
            inner = bdot(c, high)
        else:
            last = cum_ref[pl.ds(GROUP - 8, 8), :]
            factor = spread(jnp.exp(last), heads)[7:8]
            state = factor * high.astype(F32) + st_ref[...]
            hi, lo = split_two(state)
            inner = bdot(c, hi) + bdot(c, lo)
        out.append((r, y_ref[r, :] + inner * grown_ref[r, :]))
    return out


def squares(v):
    sq = v * v
    part = sum(sq[:, k : k + 128] for k in range(128, v.shape[1], 128)) + sq[:, :128]
    return exact_dot(jnp.ones((8, 128), F32), part, NT)


def gate_body(bc_ref, cum_ref, prev_ref, st_ref, y_ref, grown_ref, silu_ref, gain, g_ref, ss_ref):
    for r, mixed in mixed_blocks(bc_ref, cum_ref, prev_ref, st_ref, y_ref, grown_ref):
        gated = mixed * silu_ref[r, :]
        g_ref[r, :] = (gated * gain).astype(BF16)
        ss_ref[:, r] = squares(gated)


def last_body(bc_ref, cum_ref, prev_ref, st_ref, y_ref, grown_ref, m_ref, ss_ref):
    for r, mixed in mixed_blocks(bc_ref, cum_ref, prev_ref, st_ref, y_ref, grown_ref):
        m_ref[r, :] = mixed
        ss_ref[:, r] = squares(mixed)


NC = 8
CHUNK_LAG = 2
MESH = pl.DeviceIdType.MESH
Y, Z, CORES = 4, 8, 2


def place():
    seq = lax.axis_index("seq")
    return seq // (Z * CORES), (seq // CORES) % Z, seq % CORES


def seq_of(y, z, c):
    return (y * Z + z) * CORES + c


class Copies:
    def __init__(self, send_sem, recv_sem):
        self.send_sem, self.recv_sem = send_sem, recv_sem
        self.names = {}
        self.started = []

    def _make(self, name, src, dst, device):
        at = self.names.setdefault(name, len(self.names))
        return pltpu.make_async_remote_copy(
            src_ref=src, dst_ref=dst, send_sem=self.send_sem.at[at], recv_sem=self.recv_sem.at[at],
            device_id=device, device_id_type=MESH,
        )

    def send(self, name, src, dst, device):
        copy = self._make(name, src, dst, device)
        copy.start()
        self.started.append(copy)

    def arrived(self, name, where, device):
        self._make(name, where, where, device).wait_recv()

    def finish(self):
        for copy in self.started:
            copy.wait_send()


def weight_steps(cp, tag, own, w, local_sem, a_rows):
    y, z, c = place()
    head = lax.axis_index("head")
    f = 1 - 2 * c
    top, low = pl.ds(0, a_rows), pl.ds(a_rows, own.shape[0] - a_rows)

    def at_y(k):
        return lax.rem(y + k * f + 2 * Y, Y)

    def at_z(k):
        return lax.rem(z + k * f + 2 * Z, Z)

    to_y = {k: (seq_of(at_y(k), z, c), head) for k in (1, -1)}
    to_z = {k: (seq_of(y, at_z(k), c), head) for k in (1, -1)}
    other = (seq_of(y, z, 1 - c), head)

    def a_piece(ky):
        return w.at[at_y(ky), z, c, top]

    def a_block(kz):
        return w.at[:, at_z(kz), c, top]

    def b_piece(ky, kz):
        return w.at[at_y(ky), at_z(kz), c, low]

    def push(name, ref, device):
        cp.send((tag, *name), ref, ref, device)

    def here(name, ref, device):
        cp.arrived((tag, *name), ref, device)

    def a_share(kz):
        push(("as", kz), a_block(kz), other)

    def b_share(ky, kz):
        push(("bs", ky, kz), b_piece(ky, kz), other)

    def a_went(way, k):
        kz = -way * (k + 1)
        here(("az", way, k), a_block(kz), to_z[way])
        if k < (3 if way == 1 else 2):
            push(("az", way, k + 1), a_block(kz), to_z[way])
        a_share(kz)

    def b_went(way, k):
        kz = -way * (k + 1)
        here(("bz", way, k), b_piece(0, kz), to_z[way])
        if k < (3 if way == -1 else 2):
            push(("bz", way, k + 1), b_piece(0, kz), to_z[way])
        for along in (-1, 1):
            push(("by", along, kz), b_piece(0, kz), to_y[along])
        b_share(0, kz)

    def b_on(kz):
        here(("by", -1, kz), b_piece(1, kz), to_y[-1])
        push(("bf", kz), b_piece(1, kz), to_y[-1])
        b_share(1, kz)
        here(("by", 1, kz), b_piece(-1, kz), to_y[1])
        b_share(-1, kz)

    def b_end(kz):
        here(("bf", kz), b_piece(2, kz), to_y[-1])
        b_share(2, kz)

    def s0():
        mine = pltpu.make_async_copy(own, w.at[y, z, c], local_sem)
        mine.start()
        for way in (1, -1):
            cp.send((tag, "ay", way, 0), own.at[top], a_piece(0), to_y[way])
            cp.send((tag, "bz", way, 0), own.at[low], b_piece(0, 0), to_z[way])
        for way in (-1, 1):
            cp.send((tag, "by", way, 0), own.at[low], b_piece(0, 0), to_y[way])
        mine.wait()

    def s1():
        here(("ay", 1, 0), a_piece(-1), to_y[1])
        push(("ay", 1, 1), a_piece(-1), to_y[1])
        b_went(1, 0)
        b_went(-1, 0)

    def s2():
        b_went(1, 1)
        b_went(-1, 1)
        here(("ay", -1, 0), a_piece(1), to_y[-1])
        here(("ay", 1, 1), a_piece(-2), to_y[1])
        for way in (1, -1):
            push(("az", way, 0), a_block(0), to_z[way])
        b_on(0)
        a_share(0)
        b_share(0, 0)

    def s3():
        b_went(1, 2)
        b_went(-1, 2)
        b_on(-1)
        b_on(1)
        a_went(1, 0)
        a_went(-1, 0)

    def s4():
        b_went(-1, 3)
        b_on(-2)
        b_on(2)
        a_went(1, 1)
        a_went(-1, 1)
        b_end(0)

    def s5():
        b_on(-3)
        b_on(3)
        a_went(1, 2)
        a_went(-1, 2)
        b_end(-1)
        b_end(1)

    def s6():
        b_on(4)
        a_went(1, 3)
        b_end(-2)
        b_end(2)

    def s7():
        for kz in (-3, 3, 4):
            b_end(kz)

    def s8():
        for kz in range(-4, 4):
            here(("as", kz), w.at[:, lax.rem(z - kz * f + 2 * Z, Z), 1 - c, top], other)
        for ky in range(-1, 3):
            for kz in range(-3, 5):
                where = w.at[lax.rem(y - ky * f + 2 * Y, Y), lax.rem(z - kz * f + 2 * Z, Z), 1 - c, low]
                here(("bs", ky, kz), where, other)

    return [s0, s1, s2, s3, s4, s5, s6, s7, s8]


def prefix_steps(cp, tag, heads, end_ref, total_ref, prev_ref, p):
    y, z, c = place()
    head = lax.axis_index("head")
    other = (seq_of(y, z, 1 - c), head)
    n, width = end_ref.shape
    half, lanes, part = n // 2, width // 2, heads // 2
    to_z = {k: (seq_of(y, lax.rem(z + k, Z), c), head) for k in range(1, Z)}
    to_y = {k: (seq_of(lax.rem(y + k, Y), z, c), head) for k in range(1, Y)}
    mine = pl.ds(pl.multiple_of(c * half, half), half)
    theirs = pl.ds(pl.multiple_of((1 - c) * half, half), half)
    first = c == 0

    def cell(j):
        return pl.ds((j // 2) * 16, 16), pl.ds((j % 2) * lanes, lanes)

    def factor(log):
        return spread(jnp.exp(log), part)

    def log_of(tail):
        return tail[:, :part] + tail[:, part : 2 * part] + tail[:, 2 * part : 3 * part]

    def core_out():
        p.pair_out[pl.ds(0, half), :] = end_ref[theirs, :]
        p.pair_out[pl.ds(half, 8), pl.ds(0, 128)] = total_ref[...]
        p.pair_out[pl.ds(half, 8), pl.ds(128, width - 128)] = jnp.zeros((8, width - 128), F32)
        cp.send((tag, "out"), p.pair_out, p.pair_in, other)

    def z_out():
        cp.arrived((tag, "out"), p.pair_in, other)
        own, got = end_ref[mine, :], p.pair_in[pl.ds(0, half), :]
        own_log = total_ref[:, :heads]
        got_log = p.pair_in[pl.ds(half, 8), pl.ds(0, 128)][:, :heads]
        s0, s1 = jnp.where(first, own, got), jnp.where(first, got, own)
        log0, log1 = jnp.where(first, own_log, got_log), jnp.where(first, got_log, own_log)
        p.zero_state[...] = s0
        p.zero_factor[...] = spread(jnp.exp(log0), heads)
        chip = spread(jnp.exp(log1), heads)[0:1] * s0 + s1
        log = log0 + log1
        log = jnp.concatenate([log, log], axis=0)
        for j in range(Z):
            r, q = cell(j)
            p.z_out[j, :, pl.ds(0, lanes)] = chip[r.start : r.start + 16, q.start : q.start + lanes].astype(BF16)
            rest = log[:, (j % 2) * part : (j % 2 + 1) * part]
            pieces = []
            for _ in range(3):
                piece = rest.astype(BF16).astype(F32)
                pieces.append(piece)
                rest = rest - piece
            pieces.append(jnp.zeros((16, 128 - 3 * part), F32))
            p.z_out[j, :, pl.ds(lanes, 128)] = jnp.concatenate(pieces, axis=1).astype(BF16)
        for k in FAR_FIRST:
            cp.send((tag, "z", k), p.z_out.at[lax.rem(z + k, Z)], p.z_in.at[z], to_z[k])
        p.z_in[z] = p.z_out[z]

    def y_out():
        for k in range(1, Z):
            cp.arrived((tag, "z", k), p.z_in.at[lax.rem(z - k + Z, Z)], to_z[k])
        run = jnp.zeros((16, lanes), F32)
        logs = jnp.zeros((16, part), F32)
        every = log_of(p.z_in[:, :, pl.ds(lanes, 128)].astype(F32).reshape(Z * 16, 128))
        factors = factor(every)
        for j in range(Z):
            log, f = every[16 * j : 16 * j + 16], factors[16 * j : 16 * j + 16]
            p.z_factor[j] = f
            run = f * run + p.z_in[j, :, pl.ds(0, lanes)].astype(F32)
            logs = logs + log
        p.y_in[y, :, pl.ds(0, lanes)] = run
        p.y_in[y, :, pl.ds(lanes, 128)] = jnp.concatenate([logs, jnp.zeros((16, 128 - part), F32)], axis=1)
        for k in range(1, Y):
            cp.send((tag, "y", k), p.y_in.at[y], p.y_in.at[y], to_y[k])

    def z_back():
        for k in range(1, Y):
            cp.arrived((tag, "y", k), p.y_in.at[lax.rem(y - k + Y, Y)], to_y[k])
        run = jnp.zeros((16, lanes), F32)
        factors = factor(p.y_in[:, :, pl.ds(lanes, 128)].reshape(Y * 16, 128)[:, :part])
        for j in range(Y):
            f = factors[16 * j : 16 * j + 16]
            run = jnp.where(j < y, f * run + p.y_in[j, :, pl.ds(0, lanes)], run)
        for j in range(Z):
            p.back_out[j] = run.astype(BF16)
            run = p.z_factor[j] * run + p.z_in[j, :, pl.ds(0, lanes)].astype(F32)
        for k in FAR_FIRST:
            cp.send((tag, "b", k), p.back_out.at[lax.rem(z + k, Z)], p.back_in.at[z], to_z[k])
        p.back_in[z] = p.back_out[z]

    def core_back():
        for k in range(1, Z):
            cp.arrived((tag, "b", k), p.back_in.at[lax.rem(z - k + Z, Z)], to_z[k])
        rows = [
            jnp.concatenate([p.back_in[2 * i], p.back_in[2 * i + 1]], axis=1) for i in range(Z // 2)
        ]
        zero = jnp.concatenate(rows, axis=0).astype(F32)
        one = p.zero_factor[0:1, :] * zero + p.zero_state[...]
        p.core_out[...] = jnp.where(first, one, zero).astype(BF16)
        cp.send((tag, "core"), p.core_out, prev_ref.at[mine], other)
        prev_ref[mine, :] = jnp.where(first, zero, one).astype(BF16)

    def done():
        cp.arrived((tag, "core"), prev_ref.at[theirs], other)

    return [core_out, z_out, y_out, z_back, core_back, done], [*to_z.values(), *to_y.values(), other]


FAR_FIRST = sorted(range(1, Z), key=lambda k: -min(k, Z - k))
N_PREFIX_COPIES = 2 * Z + Y - 1


N_WEIGHT_COPIES = 53 + 28


def greet(devices):
    barrier = pltpu.get_barrier_semaphore()
    for device in devices:
        pl.semaphore_signal(barrier, inc=1, device_id=device, device_id_type=MESH)
    pl.semaphore_wait(barrier, len(devices))


def mixer_body(names, *refs):
    a = types.SimpleNamespace(**dict(zip(names, refs)))
    rows, width = a.x_in.shape
    heads = a.step_in.shape[0]
    states = a.bc_in.shape[1]
    seq, me = lax.axis_index("seq"), lax.axis_index("head")
    n_seq, n_head = lax.axis_size("seq"), lax.axis_size("head")
    depth = width * n_head
    r, o, l = (lax.rem(me + k, n_head) for k in (1, 2, 3))
    right, opposite, left = ((seq, k) for k in (r, o, l))
    after, before = ((lax.rem(seq + k, n_seq), me) for k in (1, n_seq - 1))
    across = ((1, right), (2, opposite), (3, left))
    cp = Copies(a.send_sem, a.recv_sem)
    out_steps = weight_steps(cp, "wo", a.w_out, a.wo, a.local_sem.at[0], 16)
    steps = weight_steps(cp, "wi", a.wi_own, a.wi, a.local_sem.at[1], 32)

    def prefix_of(layer):
        views = {k: getattr(a, k).at[layer] for k in PREFIX_NAMES}
        return prefix_steps(
            cp, ("prefix", layer), heads, a.end, a.total, a.prev.at[layer], types.SimpleNamespace(**views)
        )

    prefix, partners = prefix_of(0)
    loads = {
        name: pltpu.make_async_copy(getattr(a, name + "_hbm"), getattr(a, name), a.local_sem.at[2 + k])
        for k, name in enumerate(LATE)
    }
    for load in loads.values():
        load.start()
    a.wi_own[:, pl.ds(0, width)] = a.w_in_x[...]
    a.wi_own[:, pl.ds(width, states)] = a.w_in_bc[...]
    dt = a.w_in_dt[...].astype(F32).T
    dt = jnp.concatenate([dt, jnp.zeros((dt.shape[0], 128 - heads), F32)], axis=1)
    a.wi_own[:, pl.ds(width + states, 128)] = dt.astype(BF16)
    a.step_one[...] = a.step_in[...].T
    greet([right, opposite, left, after, before, *partners])

    def turn(work):
        if work:
            work.pop(0)()

    turn(out_steps)
    loads["x_in"].wait()
    loads["bc_in"].wait()

    def block_states(layer, b, x_ref, bc_ref, step_ref):
        code = a.code[layer, :, b * GROUP : (b + 1) * GROUP]
        rate = a.rate[layer : layer + 1, :]
        states_block(b, x_ref, bc_ref, step_ref, code, rate, a.st, a.end, a.total, a.cum)

    for b in range(rows // GROUP):
        block_states(0, b, a.x_in, a.bc_in, a.step_one)
    turn(prefix)
    turn(out_steps)
    diag = diag_pieces(a.x_in, a.bc_in, a.step_one, a.cum, a.skip[0:1, :], a.own)
    def grow():
        a.left[...] = spread(jnp.exp(a.cum[...]), heads)

    def silu():
        loads["gate"].wait()
        gate = a.gate[...].astype(F32)
        a.right[...] = gate / (1.0 + jnp.exp(-gate))
        grow()

    diag.append(silu)
    while prefix:
        turn(diag)
        turn(prefix)
        turn(out_steps)
    loads["resid_in"].wait()
    gate_body(a.bc_in, a.cum, a.prev.at[0], a.st, a.own, a.left, a.right, a.norm_gain[...], a.g, a.ss.at[0])
    for k, device in across:
        cp.send(("ss", k), a.ss.at[0], a.ss_in.at[k - 1], device)
    while len(out_steps) > 1:
        turn(out_steps)
    turn(steps)
    turn(out_steps)

    g_ref, wo_ref, resid_ref, gain_ref, bias_ref = a.g, a.wo, a.resid_in, a.resid_gain, a.bias
    cx_ref, cbc_ref, out_ref, x_ref, bc_ref, step_ref = a.conv_x, a.conv_bc, a.resid_out, a.x_two, a.bc_two, a.step_two
    w_ref, hid_ref, h_ref, opp_ref, right_ref, left_ref, own_ref = a.wi, a.hid, a.h, a.opp, a.right, a.left, a.own
    sum_r_ref, sum_l_ref, in_l1, in_r1, in_l2, in_r2 = a.sum_r, a.sum_l, a.in_l1, a.in_r1, a.in_l2, a.in_r2
    ss_ref, ss_in, tail_ref, halo_ref, scale_ref, rs_ref, pre_ref = (
        a.ss.at[0], a.ss_in, a.tail, a.halo, a.scale, a.rs, a.pre
    )
    chunk = rows // NC
    half = width // 2
    lo, hi = pl.ds(0, half), pl.ds(half, half)
    order = [NC - 1, *range(NC - 1)]
    tile = 256

    def cut(c):
        return pl.ds(c * chunk, chunk)

    def product(dest, store):
        @pl.loop(0, width // tile)
        def _(j):
            at = pl.multiple_of(j * tile, tile)
            weight = wo_ref[dest, pl.ds(j * (Z // 4), Z // 4)].reshape(tile, width)
            store(pl.ds(at, tile), bdot(g_ref[...], weight, NT))

    def project():
        def to_opp(cols, p):
            opp_ref[:, cols] = p.astype(BF16)

        def keep(ref):
            def store(cols, p):
                ref[:, cols] = p

            return store

        product(o, to_opp)
        for c in order:
            cp.send(("1r", c), opp_ref.at[cut(c), lo], in_l1.at[cut(c)], right)
            cp.send(("1l", c), opp_ref.at[cut(c), hi], in_r1.at[cut(c)], left)
        product(r, keep(right_ref))
        product(l, keep(left_ref))
        product(me, keep(own_ref))

    def second_sum(c):
        q = cut(c)
        cp.arrived(("1r", c), in_l1.at[q], right)
        sum_r_ref[q, lo] = (right_ref[q, lo] + in_l1[q, :].astype(F32)).astype(BF16)
        sum_r_ref[q, hi] = right_ref[q, hi].astype(BF16)
        cp.send(("2r", c), sum_r_ref.at[q], in_l2.at[q], right)
        cp.arrived(("1l", c), in_r1.at[q], left)
        sum_l_ref[q, hi] = (left_ref[q, hi] + in_r1[q, :].astype(F32)).astype(BF16)
        sum_l_ref[q, lo] = left_ref[q, lo].astype(BF16)
        cp.send(("2l", c), sum_l_ref.at[q], in_r2.at[q], left)

    def token_scale(tag, ss_ref, ss_in):
        for k, device in across:
            cp.arrived((tag, k), ss_in.at[k - 1], device)
        total = ss_ref[...] + ss_in[0] + ss_in[1] + ss_in[2]
        eighth = jnp.full((8, 128), 0.125, F32)
        column = exact_dot(total, eighth, (((0,), (0,)), ((), ())))
        scale_ref[...] = lax.rsqrt(column / depth + 1e-05)

    def residual(c):
        q = cut(c)
        cp.arrived(("2r", c), in_l2.at[q], right)
        cp.arrived(("2l", c), in_r2.at[q], left)
        total = own_ref[q, :] + in_l2[q, :].astype(F32) + in_r2[q, :].astype(F32)
        total = total * scale_ref[q, 0:1] + resid_ref[q, :].astype(F32)
        out_ref[q, :] = total.astype(BF16)
        hid_ref[me, q, :] = out_ref[q, :]
        cp.send(("3r", c), hid_ref.at[me, q], hid_ref.at[me, q], right)
        cp.send(("3l", c), hid_ref.at[me, q], hid_ref.at[me, q], left)

    def hand_on(c):
        q = cut(c)
        cp.arrived(("3r", c), hid_ref.at[l, q], right)
        cp.send(("4r", c), hid_ref.at[l, q, lo], hid_ref.at[l, q, lo], right)
        cp.arrived(("3l", c), hid_ref.at[r, q], left)
        cp.send(("4l", c), hid_ref.at[r, q, hi], hid_ref.at[r, q, hi], left)

    def scaled(src, q, at, n, keep):
        parts = [src[k, q, :].astype(F32) for k in range(n_head)]
        total = sum(jnp.sum(v * v, axis=1, keepdims=True) for v in parts)
        rs = lax.rsqrt(total / depth + 1e-05)
        rs_ref[pl.ds(at, n), :] = jnp.broadcast_to(rs if keep is None else rs * keep, (n, 128))
        for k, v in enumerate(parts):
            h_ref[k, pl.ds(at, n), :] = (v * gain_ref[:, k * width : (k + 1) * width]).astype(BF16)

    def complete(c):
        q = cut(c)
        cp.arrived(("4r", c), hid_ref.at[o, q, lo], right)
        cp.arrived(("4l", c), hid_ref.at[o, q, hi], left)
        if c == NC - 1:
            tail_ref[...] = hid_ref[:, pl.ds(rows - HALO, HALO), :]
            cp.send("halo", tail_ref, halo_ref, after)
        scaled(hid_ref, q, c * chunk + HALO, chunk, None)

    def into(cols, at, n):
        total = None
        for k in range(n_head):
            piece = bdot(
                h_ref[k, pl.ds(at, n), :], w_ref[k, :, :, :, cols].reshape(width, cols.size)
            )
            total = piece if total is None else total + piece
        return total

    def conv(taps, k):
        n = taps.shape[1]
        total = None
        for tap in range(k):
            v = pre_ref[pl.ds(HALO - k + 1 + tap, GROUP), :n] * taps[tap : tap + 1, :].astype(F32)
            total = v if total is None else total + v
        return (total / (1.0 + jnp.exp(-total))).astype(BF16)

    def second_inputs(b):
        at, every = b * GROUP, GROUP + HALO
        r = pl.ds(at, GROUP)

        def pre(cols):
            rs = rs_ref[pl.ds(at, every), :]
            both = jnp.concatenate([rs, rs], axis=1)
            pre_ref[...] = (into(cols, at, every) * both).astype(BF16).astype(F32)

        @pl.loop(0, width // tile)
        def _(i):
            cols = pl.ds(pl.multiple_of(i * tile, tile), tile)
            pre(cols)
            x_ref[r, cols] = conv(cx_ref[:, cols], cx_ref.shape[0])

        pre(pl.ds(width, states))
        bc_ref[r, :] = conv(cbc_ref[...], cbc_ref.shape[0])
        dt = into(pl.ds(width + states, 128), at + HALO, GROUP)
        dt = (dt * rs_ref[pl.ds(at + HALO, GROUP), :])[:, :heads] + bias_ref[...]
        step_ref[r, :] = jnp.maximum(dt, 0.0) + jnp.log(1.0 + jnp.exp(-jnp.abs(dt)))

    diag = diag_pieces(x_ref, bc_ref, step_ref, a.cum, a.skip[1:2, :], a.right)

    def first_block(t):
        if t == 4 + 3 * CHUNK_LAG:
            cp.arrived("halo", halo_ref, after)
            scaled(halo_ref, pl.ds(0, HALO), 0, HALO, jnp.where(seq == 0, 0.0, 1.0))
            while steps:
                turn(steps)
            second_inputs(0)
        if t == 5 + 3 * CHUNK_LAG:
            block_states(1, 0, x_ref, bc_ref, step_ref)
        if t >= 6 + 3 * CHUNK_LAG:
            turn(diag)

    project()
    for t in range(NC + 3 * CHUNK_LAG):
        for stage, work in reversed(list(enumerate((second_sum, residual, hand_on, complete)))):
            k = t - CHUNK_LAG * stage
            if 0 <= k < NC:
                if work is residual and k == 0:
                    token_scale("ss", ss_ref, ss_in)
                work(order[k])
        if t >= 1:
            turn(steps)
        first_block(t)
    second_inputs(1)
    block_states(1, 1, x_ref, bc_ref, step_ref)
    prefix, _ = prefix_of(1)
    turn(prefix)
    diag.append(grow)
    while prefix:
        turn(diag)
        turn(prefix)
    last_body(bc_ref, a.cum, a.prev.at[1], a.st, a.right, a.left, a.left, a.ss.at[1])
    for k, device in across:
        cp.send(("ss two", k), a.ss.at[1], a.ss_two.at[k - 1], device)
    token_scale("ss two", a.ss.at[1], a.ss_two)
    for c in range(NC):
        q = cut(c)
        a.mixer_out[q, :] = (a.left[q, :] * scale_ref[q, 0:1]).astype(BF16)
    cp.finish()


PARTS = 8


def place_body(one_ref, two_ref, one_out, two_out, sem):
    step = one_ref.shape[0] // PARTS
    copies = [
        pltpu.make_async_copy(src.at[pl.ds(k * step, step)], dst.at[pl.ds(k * step, step)], sem.at[i, k])
        for k in range(PARTS)
        for i, (src, dst) in enumerate(((one_ref, one_out), (two_ref, two_out)))
    ]
    for copy in copies:
        copy.start()
    for copy in copies:
        copy.wait()


LATE = ("x_in", "bc_in", "gate", "resid_in")
PREFIX_NAMES = (
    "pair_out", "pair_in", "zero_state", "zero_factor", "z_out", "z_in", "z_factor", "y_in", "back_out", "back_in", "core_out",
)


def mixer(ins, rows, width, heads, states):
    n_head = lax.axis_size("head")
    n = states // 2
    lanes = width // 2
    copies = 2 * N_WEIGHT_COPIES + 2 * N_PREFIX_COPIES + 6 + 1 + 8 * NC
    outs = {"resid_out": sds(rows, width, dtype=BF16), "mixer_out": sds(rows, width, dtype=BF16)}

    def keep(*shape, dtype=F32):
        return pltpu.VMEM(shape, dtype)

    small = functools.partial(keep, dtype=BF16)
    scratch = {
        "wo": small(Y, Z, CORES, *ins["w_out"].shape),
        "wi": small(Y, Z, CORES, ins["w_in_x"].shape[0], width + states + 128),
        "hid": small(n_head, rows, width),
        "h": small(n_head, rows + HALO, width),
        "opp": small(rows, width),
        "right": keep(rows, width),
        "left": keep(rows, width),
        "own": keep(rows, width),
        "sum_r": small(rows, width),
        "sum_l": small(rows, width),
        "in_l1": small(rows, lanes),
        "in_r1": small(rows, lanes),
        "in_l2": small(rows, width),
        "in_r2": small(rows, width),
        "g": small(rows, width),
        "x_two": small(rows, width),
        "bc_two": small(rows, states),
        "step_two": keep(rows, heads),
        "cum": keep(rows, heads),
        "st": keep(n, width),
        "end": keep(n, width),
        "total": keep(8, 128),
        "prev": small(2, n, width),
        "ss": keep(2, 8, rows),
        "ss_in": keep(3, 8, rows),
        "ss_two": keep(3, 8, rows),
        "tail": small(n_head, HALO, width),
        "halo": small(n_head, HALO, width),
        "scale": keep(rows, 128),
        "rs": keep(rows + HALO, 128),
        "pre": keep(GROUP + HALO, 256),
        "wi_own": small(ins["w_in_x"].shape[0], width + states + 128),
        **{name: small(*ins[name + "_hbm"].shape) for name in LATE},
        "step_one": keep(rows, heads),
        "pair_out": keep(2, n // 2 + 8, width),
        "pair_in": keep(2, n // 2 + 8, width),
        "zero_state": keep(2, n // 2, width),
        "zero_factor": keep(2, 8, width),
        "z_out": small(2, Z, 16, lanes + 128),
        "z_in": small(2, Z, 16, lanes + 128),
        "z_factor": keep(2, Z, 16, lanes),
        "y_in": keep(2, Y, 16, lanes + 128),
        "back_out": small(2, Z, 16, lanes),
        "back_in": small(2, Z, 16, lanes),
        "core_out": small(2, n // 2, width),
        "send_sem": pltpu.SemaphoreType.DMA((copies,)),
        "recv_sem": pltpu.SemaphoreType.DMA((copies,)),
        "local_sem": pltpu.SemaphoreType.DMA((2 + len(LATE),)),
    }
    return call(
        functools.partial(mixer_body, (*ins, *outs, *scratch)),
        tuple(outs.values()),
        tuple(ins.values()),
        scratch.values(),
        limit=60,
        far=[name.endswith("_hbm") for name in ins],
        collective_id=1,
        has_side_effects=True,
    )


def call(body, outs, args, scratch=(), limit=56, far=(), **kw):
    return pl.pallas_call(
        body,
        out_shape=outs,
        in_specs=[pl.BlockSpec(memory_space=pl.ANY) if k else VMEM for k in far],
        out_specs=jax.tree.map(lambda _: VMEM, outs),
        scratch_shapes=list(scratch),
        compiler_params=pltpu.CompilerParams(vmem_limit_bytes=limit * 2**20, **kw),
    )(*args)


def sds(*shape, dtype=F32):
    return jax.ShapeDtypeStruct(shape, dtype)


def on_device(
    x_in, gate_in, bc_in, step_in, decay_code, decay_rate, skip_gain, norm_gain, w_out, resid_in,
    resid_gain, w_in_x, w_in_bc, w_in_dt, step_time_bias, conv_x, conv_bc,
):
    rows, width = x_in.shape
    heads = step_in.shape[1]
    ins = {
        "x_in_hbm": x_in, "gate_hbm": gate_in, "bc_in_hbm": bc_in, "step_in": step_in.T, "code": jnp.swapaxes(decay_code, 1, 2), "rate": decay_rate,
        "skip": skip_gain, "norm_gain": norm_gain[None, :], "w_out": w_out.T, "resid_in_hbm": resid_in,
        "resid_gain": resid_gain[None, :], "w_in_x": w_in_x, "w_in_bc": w_in_bc, "w_in_dt": w_in_dt.T, "bias": step_time_bias[None, :], "conv_x": conv_x,
        "conv_bc": conv_bc,
    }
    outs = mixer(ins, rows, width, heads, bc_in.shape[1])
    anywhere = pl.BlockSpec(memory_space=pl.ANY)
    return pl.pallas_call(
        place_body,
        out_shape=tuple(sds(*v.shape, dtype=v.dtype) for v in outs),
        in_specs=[anywhere] * 2,
        out_specs=(anywhere,) * 2,
        scratch_shapes=[pltpu.SemaphoreType.DMA((2, PARTS))],
        compiler_params=pltpu.CompilerParams(vmem_limit_bytes=62 * 2**20),
    )(*outs)


def solution(mesh):
    in_specs = (
        P("seq", "head"), P("seq", "head"), P("seq", None), P("seq", "head"), P(None, "seq", "head"),
        P(None, "head"), P(None, "head"), P("head"), P("head", "seq"), P("seq", "head"), P(),
        P("seq", "head"), P("seq", None), P("seq", "head"), P("head"), P(None, "head"), P(),
    )
    out_specs = (P("seq", "head"), P("seq", "head"))
    return jax.shard_map(
        on_device, mesh=mesh, in_specs=in_specs, out_specs=out_specs, check_vma=False
    )
```
